512 devices in a mesh: tm: 128 (over y_hi, z, x), rows: 4 (over y_lo, core).
Axes of the slice: x: 4, y: 4 (y_hi: 2, y_lo: 2; y = y_hi * 2 + y_lo), z: 16, core: 2. Of those that a mesh axis runs over, the one named last changes fastest.
Arguments:
- latents: bfloat16 [128, 16, 32, 640], P('tm', 'rows'), may hold values from -20 to 20
- gn_gain: float32 [640], replicated, may hold values from 0.5 to 2
- conv_weight: bfloat16 [9, 640, 640], P(None, 'rows'), may hold values from -0.078125 to 0.078125
- conv_bias: float32 [640], replicated, may hold values from -3 to 3
- ln_gain: float32 [640], replicated, may hold values from 0.5 to 2
- qkv_weight: bfloat16 [640, 1920], P('rows'), may hold values from -1.5 to 1.5
Outputs:
- restyled: bfloat16 [128, 16, 32, 640], P('tm', 'rows')
The draws below stay inside these ranges and needn't reach their ends.
All inputs are finite; a program needn't handle non-finite values.
Results may differ from the reference program's by a relative error of at most 0.023.
Values may be sent and summed in bfloat16 or wider, within the bound.
No kernel may reach another device: no remote copies, remote signals or barrier semaphores. Data moves between devices by JAX's collectives and lax.ppermute only.
A program may use at most 64 MiB of HBM per device.

```python
import math
import jax
import jax.numpy as jnp
from jax import lax

C = 640
HEADS = 8
GROUPS = 32
LAT_W = 32
FRAMES = 128
LAT_H = 16


def draw_latents(key, part):
    key = jax.random.fold_in(key, 11)
    first = jax.random.fold_in(key, 0)
    second = jax.random.fold_in(key, 1)
    third = jax.random.fold_in(key, 2)
    fifth = jax.random.fold_in(key, 4)
    sixth = jax.random.fold_in(key, 5)
    shape = (FRAMES, LAT_H, LAT_W, C)
    position = jnp.arange(LAT_H, dtype=jnp.float32) / (LAT_H - 1)
    ramp = jnp.exp(position * math.log(3.0))
    jitter = jnp.exp(jax.random.uniform(second, (LAT_H,), jnp.float32) * math.log(3.0))
    row_scale = ramp * jitter / 3.0
    chan_scale = jnp.exp(jax.random.uniform(third, (C,), jnp.float32) * math.log(10.0)) / math.sqrt(10.0)
    group_sign = jnp.where(jax.random.bernoulli(fifth, 0.5, (GROUPS,)), 1.0, -1.0).astype(jnp.float32)
    chan_level = jnp.repeat(group_sign, C // GROUPS) * (0.7 + 0.6 * jax.random.uniform(sixth, (C,), jnp.float32))
    base = jax.random.normal(first, shape, jnp.float32)
    offset_ramp = jnp.exp(position * math.log(3.0)) / 3.0
    offset = 1.5 * offset_ramp[:, None] * chan_level[None, :]
    values = base * row_scale[None, :, None, None] * chan_scale[None, None, None, :] + offset[None, :, None, :]
    return jnp.clip(values, -20.0, 20.0).astype(jnp.bfloat16)


def draw_qkv_weight(key, part):
    key = jax.random.fold_in(key, 23)
    first, second, third = jax.random.split(key, 3)
    base_q = jax.random.normal(first, (C, C), jnp.float32)
    base_k = jax.random.normal(second, (C, C), jnp.float32)
    base_v = jax.random.normal(third, (C, C), jnp.float32)
    root = math.sqrt(C)
    w_query = 1.5 * base_q / root
    w_key = 1.5 * base_k / root
    w_value = base_v / root
    joined = jnp.concatenate([w_query, w_key, w_value], axis=1)
    return jnp.clip(joined, -1.5, 1.5).astype(jnp.bfloat16)


def steps_of(key, extent, pieces, least, largest):
    gain, own = 1.0, jax.random.fold_in(key, 6)
    for axis_at, shards_of in pieces:
        heights = jnp.exp(jax.random.uniform(jax.random.fold_in(own, axis_at), (shards_of,), jnp.float32, least / len(pieces), largest / len(pieces)))
        gain = gain * jnp.repeat(heights, extent[axis_at] // shards_of).reshape([-1 if axis == axis_at else 1 for axis in range(len(extent))])
    return gain


def noise(key, shape, scale, reach, cuts=(), kind=jnp.bfloat16):
    drawn = scale * jax.random.normal(key, shape, jnp.float32)
    if cuts:
        drawn = drawn * steps_of(key, shape, cuts, -0.22, 0.18)
    return jnp.clip(drawn, -reach, reach).astype(kind)


def setup_inputs(seed: int = 0) -> dict:
    streams_of = jax.random.split(jax.random.key(seed), 7)
    latents = draw_latents(jax.random.fold_in(streams_of[6], 71), 0)
    gn_gain = jnp.clip(jnp.exp(jax.random.uniform(streams_of[1], (C,), jnp.float32, math.log(0.5), math.log(2.0))), 0.5, 2.0)
    conv_weight = noise(streams_of[2], (9, C, C), (9 * C) ** -0.5, 0.078125, ((1, 4),))
    conv_bias = noise(streams_of[3], (C,), 0.5, 3.0, (), jnp.float32)
    ln_gain = jnp.clip(jnp.exp(jax.random.uniform(streams_of[4], (C,), jnp.float32, math.log(0.5), math.log(2.0))), 0.5, 2.0)
    qkv_weight = draw_qkv_weight(jax.random.fold_in(streams_of[6], 71), 0)
    return dict(latents=latents, gn_gain=gn_gain, conv_weight=conv_weight, conv_bias=conv_bias, ln_gain=ln_gain, qkv_weight=qkv_weight)


EPS = 1e-05

def frame_block(frame, gn_gain, conv_weight, conv_bias, ln_gain, qkv_weight):
    height, width, chans = frame.shape
    group_size = chans // GROUPS
    values = frame.astype(jnp.float32).reshape(height * width, GROUPS, group_size)
    mean = lax.optimization_barrier(jnp.mean(values, axis=(0, 2)))
    centred = values - mean[None, :, None]
    spread = lax.optimization_barrier(jnp.mean(centred * centred, axis=(0, 2)))
    normed = (centred * lax.rsqrt(spread + EPS)[None, :, None]).reshape(height, width, chans) * gn_gain
    act = jax.nn.silu(normed).astype(jnp.bfloat16)
    padded = jnp.pad(act, ((1, 1), (1, 1), (0, 0)))
    conv = jnp.zeros((height * width, chans), jnp.float32)
    for row_tap in range(3):
        for col_tap in range(3):
            window = padded[row_tap:row_tap + height, col_tap:col_tap + width, :].reshape(height * width, chans)
            conv = conv + jnp.dot(window, conv_weight[3 * row_tap + col_tap], preferred_element_type=jnp.float32)
    residual = (frame.astype(jnp.float32).reshape(height * width, chans) + conv + conv_bias).astype(jnp.bfloat16)
    rfloat = residual.astype(jnp.float32)
    centre = lax.optimization_barrier(jnp.mean(rfloat, axis=1, keepdims=True))
    dev = rfloat - centre
    var = lax.optimization_barrier(jnp.mean(dev * dev, axis=1, keepdims=True))
    feats = (dev * lax.rsqrt(var + EPS) * ln_gain).astype(jnp.bfloat16)
    proj = jnp.dot(feats, qkv_weight, preferred_element_type=jnp.float32)
    query = proj[:, :chans].astype(jnp.bfloat16)
    keys = proj[:, chans:2 * chans].astype(jnp.bfloat16)
    vals = proj[:, 2 * chans:].astype(jnp.bfloat16)
    return (residual, query, keys, vals)

def reference(latents, gn_gain, conv_weight, conv_bias, ln_gain, qkv_weight):
    frames, height, width, chans = latents.shape
    head_dim = chans // HEADS
    scale = head_dim ** (-0.5)

    def one_frame(frame):
        return frame_block(frame, gn_gain, conv_weight, conv_bias, ln_gain, qkv_weight)
    residual, query, keys, vals = lax.map(one_frame, latents)
    cells = height * width

    def attend_frame(index):
        prev = jnp.maximum(index - 1, 0).astype(jnp.int32)
        key_set = jnp.concatenate([keys[0], lax.dynamic_index_in_dim(keys, prev, 0, keepdims=False)], 0)
        val_set = jnp.concatenate([vals[0], lax.dynamic_index_in_dim(vals, prev, 0, keepdims=False)], 0)
        qrow = lax.dynamic_index_in_dim(query, index, 0, keepdims=False)
        qh = qrow.astype(jnp.float32).reshape(cells, HEADS, head_dim)
        kh = key_set.astype(jnp.float32).reshape(2 * cells, HEADS, head_dim)
        vh = val_set.astype(jnp.float32).reshape(2 * cells, HEADS, head_dim)
        scores = jnp.einsum('phd,khd->hpk', qh, kh) * scale
        top = lax.optimization_barrier(jnp.max(scores, axis=-1, keepdims=True))
        weights = jnp.exp(scores - top)
        den = lax.optimization_barrier(jnp.sum(weights, axis=-1))
        rounded = lax.optimization_barrier(weights.astype(jnp.bfloat16)).astype(jnp.float32)
        mixed = jnp.einsum('hpk,khd->hpd', rounded, vh) / den[..., None]
        attn = jnp.transpose(mixed, (1, 0, 2)).reshape(cells, chans)
        resid = lax.dynamic_index_in_dim(residual, index, 0, keepdims=False)
        out = (resid.astype(jnp.float32) + attn).astype(jnp.bfloat16)
        return out.reshape(height, width, chans)
    return lax.map(attend_frame, jnp.arange(frames, dtype=jnp.int32))
```

```python
import jax
import jax.numpy as jnp
from jax import lax
from jax.sharding import PartitionSpec as P

HEADS = 8
GROUPS = 32


EPS = 1e-05


def extended(x, sides, width):
    for axis, dim in sides:
        devices, length = (lax.axis_size(axis), x.shape[dim])
        up = [(i, (i + 1) % devices) for i in range(devices - 1)]
        down = [(j, i) for i, j in up]
        last = lax.slice_in_dim(x, length - width, length, axis=dim)
        leading = lax.slice_in_dim(x, 0, width, axis=dim)
        before = lax.ppermute(last, axis, up)
        after = lax.ppermute(leading, axis, down)
        x = jnp.concatenate([before, x, after], axis=dim)
    return x


def broadcast(value, axis):
    devices = lax.axis_size(axis)
    me = lax.axis_index(axis)
    step = devices // 2
    while step:
        route = [(i, i + step) for i in range(0, devices, 2 * step)]
        came = lax.ppermute(value, axis, route)
        value = jnp.where(me % (2 * step) == step, came, value)
        step //= 2
    return value


def shifted(block, axis, distance):
    devices = range(lax.axis_size(axis))
    route = [(i - distance, i) for i in devices if i - distance in devices]
    return lax.ppermute(block, axis, route)


def conv_taps(padded, weights):
    height = padded.shape[1] - 2
    width = padded.shape[2] - 2
    count = weights.shape[1]
    total = jnp.zeros((padded.shape[0] * height * width, weights.shape[2]), jnp.float32)
    for row_tap in range(3):
        for col_tap in range(3):
            window = padded[:, row_tap : row_tap + height, col_tap : col_tap + width, :].reshape(
                -1, count
            )
            total = total + jnp.dot(
                window, weights[3 * row_tap + col_tap], preferred_element_type=jnp.float32
            )
    return total


def on_device(latents, gn_gain, conv_weight, conv_bias, ln_gain, qkv_weight):
    frames, rows_dev, width, chans = latents.shape
    group_size = chans // GROUPS
    row_devices = lax.axis_size("rows")
    height = rows_dev * row_devices
    count = height * width * group_size
    cells = rows_dev * width
    values = latents.astype(jnp.float32).reshape(frames, cells, GROUPS, group_size)
    total = lax.psum(jnp.sum(values, axis=(1, 3)), "rows")
    mean = total / count
    centred = values - mean[:, None, :, None]
    spread = lax.psum(jnp.sum(centred * centred, axis=(1, 3)), "rows") / count
    normed = (centred * lax.rsqrt(spread + EPS)[:, None, :, None]).reshape(
        frames, rows_dev, width, chans
    ) * gn_gain
    act = jax.nn.silu(normed).astype(jnp.bfloat16)
    padded = extended(act, (("rows", 1),), 1)
    padded = jnp.pad(padded, ((0, 0), (0, 0), (1, 1), (0, 0)))
    conv = conv_taps(padded, lax.all_gather(conv_weight, "rows", axis=1, tiled=True))
    residual = (
        latents.astype(jnp.float32).reshape(frames * cells, chans) + conv + conv_bias
    ).astype(jnp.bfloat16)
    rfloat = residual.astype(jnp.float32)
    centre = jnp.mean(rfloat, axis=1, keepdims=True)
    deviation = rfloat - centre
    variance = jnp.mean(deviation * deviation, axis=1, keepdims=True)
    feats = (deviation * lax.rsqrt(variance + EPS) * ln_gain).astype(jnp.bfloat16)
    proj = jnp.dot(
        feats,
        lax.all_gather(qkv_weight, "rows", axis=0, tiled=True),
        preferred_element_type=jnp.float32,
    )
    query = proj[:, :chans].astype(jnp.bfloat16).reshape(frames, cells, chans)
    keys = proj[:, chans : 2 * chans].astype(jnp.bfloat16).reshape(frames, cells, chans)
    vals = proj[:, 2 * chans :].astype(jnp.bfloat16).reshape(frames, cells, chans)
    anchor = broadcast(jnp.concatenate([keys[0], vals[0]], axis=1), "tm")
    anchor_keys, anchor_vals = (anchor[:, :chans], anchor[:, chans:])
    moved_keys, moved_vals = shifted((keys[frames - 1], vals[frames - 1]), "tm", 1)
    leading = lax.axis_index("tm") == 0
    moved_keys = jnp.where(leading, keys[0], moved_keys)
    moved_vals = jnp.where(leading, vals[0], moved_vals)
    prev_keys = jnp.concatenate([moved_keys[None], keys[: frames - 1]], 0)
    prev_vals = jnp.concatenate([moved_vals[None], vals[: frames - 1]], 0)
    head_dim = chans // HEADS
    scale = head_dim ** (-0.5)
    query_heads = query.reshape(frames, cells, HEADS, head_dim).transpose(2, 0, 1, 3)
    start_state = (
        jnp.full((HEADS, frames, cells), -jnp.inf, jnp.float32),
        jnp.zeros((HEADS, frames, cells), jnp.float32),
        jnp.zeros((HEADS, frames, cells, head_dim), jnp.float32),
    )
    piece_ak = lax.all_gather(anchor_keys[None], "rows", axis=1, tiled=True)
    piece_av = lax.all_gather(anchor_vals[None], "rows", axis=1, tiled=True)
    piece_pk = lax.all_gather(prev_keys, "rows", axis=1, tiled=True)
    piece_pv = lax.all_gather(prev_vals, "rows", axis=1, tiled=True)
    span = piece_pk.shape[1]
    key_all = jnp.concatenate([piece_ak, piece_pk], 1)
    val_all = jnp.concatenate([piece_av, piece_pv], 1)
    key_heads = key_all.reshape(frames, 2 * span, HEADS, head_dim).transpose(2, 0, 1, 3)
    val_heads = val_all.reshape(frames, 2 * span, HEADS, head_dim).transpose(2, 0, 1, 3)

    def one_head(item):
        q_head, k_head, v_head, top_old, den_old, acc_old = item
        scores = (
            jnp.einsum("fpd,fkd->fpk", q_head, k_head, preferred_element_type=jnp.float32) * scale
        )
        top_new = jnp.maximum(top_old, jnp.max(scores, axis=-1))
        weights = jnp.exp(scores - top_new[..., None])
        factor = jnp.exp(top_old - top_new)
        den_new = den_old * factor + jnp.sum(weights, axis=-1)
        acc_new = acc_old * factor[..., None] + jnp.einsum(
            "fpk,fkd->fpd", weights.astype(jnp.bfloat16), v_head, preferred_element_type=jnp.float32
        )
        return (top_new, den_new, acc_new)

    final_top, final_den, final_acc = lax.map(
        one_head, (query_heads, key_heads, val_heads) + tuple(start_state)
    )
    mixed = final_acc / final_den[..., None]
    attn = mixed.transpose(1, 2, 0, 3).reshape(frames * cells, chans)
    restyled = (residual.astype(jnp.float32) + attn).astype(jnp.bfloat16)
    return restyled.reshape(frames, rows_dev, width, chans)


def solution(mesh):
    return jax.shard_map(
        on_device,
        mesh=mesh,
        in_specs=(
            P("tm", "rows", None, None),
            P(),
            P(None, "rows", None),
            P(),
            P(),
            P("rows", None),
        ),
        out_specs=P("tm", "rows", None, None),
        check_vma=False,
    )
```

```python
import functools
import jax
import jax.numpy as jnp
from jax import lax
from jax.experimental import pallas as pl
from jax.experimental.pallas import tpu as pltpu
from jax.sharding import PartitionSpec as P

HEADS = 8
GROUPS = 32
EPS = 1e-05
BOTH = ("tm", "rows")
VMEM = pl.BlockSpec(memory_space=pltpu.VMEM)
SMEM = pl.BlockSpec(memory_space=pltpu.SMEM)


def tree_levels(devices):
    if devices == 128:
        z = [("z", s) for s in (8, 4, 2, 1)]
        x = [("x", s) for s in (2, 1)]
        y = [("y", 1)]
        size = {"y": 2, "z": 16, "x": 4}
        orders = (z + x + y, x + y + z)

        def index(at, sign):
            return (at["y"] * 16 + (sign * at["z"]) % 16) * 4 + at["x"]

    else:
        steps = []
        while 2 ** len(steps) < devices:
            steps.insert(0, ("z", 2 ** len(steps)))
        size = {"z": devices}
        orders = (steps, steps)

        def index(at, sign):
            return at["z"]

    levels = [[] for _ in orders[0]]
    for core, order in enumerate(orders):
        sign = 1 - 2 * core
        known = [{axis: 0 for axis in size}]
        for level, (axis, step) in enumerate(order):
            fresh = []
            for at in known:
                to = dict(at)
                to[axis] = at[axis] + step
                fresh.append(to)
                for chip in range(2):
                    row = chip * 2 + core
                    levels[level].append((index(at, sign) * 4 + row, index(to, sign) * 4 + row))
            known = known + fresh
    return levels


def to_rows(x, flip):
    return lax.ppermute(x, "rows", [(i, i ^ flip) for i in range(4)])


def gathered(x):
    core = to_rows(x, 1)
    chip = to_rows(x, 2)
    return x, core, chip, to_rows(chip, 1)


def conv_kernel(width, me_ref, b0, b1, b2, b3, gain, weight, pool, keep, send, x_ref, taps, acc):
    me = me_ref[0]
    blocks = (b0, b1, b2, b3)
    cells, chans = x_ref.shape
    part = cells // 4
    for flip, block in enumerate(blocks):
        at = pl.multiple_of((me ^ flip) * part, part)
        x_ref[pl.ds(at, part), :] = block[...].astype(jnp.float32)
    values = x_ref[...]

    def group_mean(column):
        wide = jnp.broadcast_to(column, (8, chans))
        out = jnp.dot(
            wide, pool[...], precision=lax.Precision.HIGHEST, preferred_element_type=jnp.float32
        )
        return out[:1]

    scale = 1.0 / (cells * (640 // GROUPS))
    mean = group_mean(jnp.sum(values, axis=0, keepdims=True)) * scale
    centred = values - mean
    spread = group_mean(jnp.sum(centred * centred, axis=0, keepdims=True)) * scale
    normed = centred * (lax.rsqrt(spread + EPS) * gain[...])
    act = normed / (1.0 + jnp.exp(-normed))
    act = act.astype(jnp.bfloat16).astype(jnp.float32)
    column = lax.broadcasted_iota(jnp.int32, (cells, 1), 0) & (width - 1)
    before = jnp.where(column == 0, 0.0, pltpu.roll(act, 1, 0))
    after = jnp.where(column == width - 1, 0.0, pltpu.roll(act, cells - 1, 0))
    taps[:width, :] = jnp.zeros((width, taps.shape[1]), jnp.bfloat16)
    taps[width + cells :, :] = jnp.zeros((width, taps.shape[1]), jnp.bfloat16)
    taps[width : width + cells, :] = jnp.concatenate([before, act, after], axis=1).astype(
        jnp.bfloat16
    )
    acc[...] = sum(
        jnp.dot(
            taps[row * width : row * width + cells, :],
            weight[row],
            preferred_element_type=jnp.float32,
        )
        for row in range(3)
    )
    for flip in range(4):
        at = pl.multiple_of((me ^ flip) * part, part)
        out = acc[pl.ds(at, part), :]
        if flip % 2 == 0:
            keep[flip // 2] = out
        else:
            send[flip // 2] = out.astype(jnp.bfloat16)


def norm_kernel(lat, kept, core, chip, bias, gain, residual, feats):
    conv = kept[0] + core[0].astype(jnp.float32) + chip[...].astype(jnp.float32)
    res = (lat[...].astype(jnp.float32) + conv + bias[...]).astype(jnp.bfloat16)
    residual[...] = res
    rfloat = res.astype(jnp.float32)
    dev = rfloat - jnp.mean(rfloat, axis=1, keepdims=True)
    var = jnp.mean(dev * dev, axis=1, keepdims=True)
    feats[...] = (dev * lax.rsqrt(var + EPS) * gain[...]).astype(jnp.bfloat16)


def head_window(head, head_dim, chans):
    low = head * head_dim // 128 * 128
    high = min(-(-(head + 1) * head_dim // 128) * 128, chans)
    lane = low + lax.broadcasted_iota(jnp.int32, (1, high - low), 1)
    inside = (lane >= head * head_dim) & (lane < (head + 1) * head_dim)
    return slice(low, high), inside


def project(blocks, weight, joined, keys, vals):
    part, chans = blocks[0].shape
    for at, block in enumerate(blocks):
        joined[at * part : (at + 1) * part, :] = block[...]
    for out, first in ((keys, chans), (vals, 2 * chans)):
        out[...] = jnp.dot(
            joined[...], weight[:, first : first + chans], preferred_element_type=jnp.float32
        ).astype(jnp.bfloat16)


def scores_of(query, keys, head, window, inside):
    q_head = jnp.where(inside, query[:, window], 0)
    return lax.dot_general(
        q_head,
        keys[:, window],
        (((1,), (1,)), ((), ())),
        preferred_element_type=jnp.float32,
    )


def prev_kernel(own, p0, p1, p2, p3, weight, query, top, den, acc, joined, keys, vals):
    part, chans = own.shape
    head_dim = chans // HEADS
    scale = head_dim ** (-0.5)
    query[...] = jnp.dot(
        own[...], weight[:, :chans], preferred_element_type=jnp.float32
    ).astype(jnp.bfloat16)
    project((p0, p1, p2, p3), weight, joined, keys, vals)
    acc[...] = jnp.zeros_like(acc)
    for head in range(HEADS):
        window, inside = head_window(head, head_dim, chans)
        s = scores_of(query, keys, head, window, inside)
        peak = jnp.max(s, axis=1, keepdims=True)
        w = jnp.exp((s - peak) * scale)
        top[:, head : head + 1] = peak
        den[:, head : head + 1] = jnp.sum(w, axis=1, keepdims=True)
        out = jnp.dot(
            w.astype(jnp.bfloat16), vals[:, window], preferred_element_type=jnp.float32
        )
        acc[:, window] = jnp.where(inside, out, acc[:, window])


def anchor_kernel(
    query, a0, a1, a2, a3, weight, top, den, acc, residual, restyled, joined, keys, vals, mixed
):
    part, chans = query.shape
    head_dim = chans // HEADS
    scale = head_dim ** (-0.5)
    project((a0, a1, a2, a3), weight, joined, keys, vals)
    for head in range(HEADS):
        window, inside = head_window(head, head_dim, chans)
        s = scores_of(query, keys, head, window, inside)
        old = top[:, head : head + 1]
        peak = jnp.maximum(old, jnp.max(s, axis=1, keepdims=True))
        factor = jnp.exp((old - peak) * scale)
        w = jnp.exp((s - peak) * scale)
        total = den[:, head : head + 1] * factor + jnp.sum(w, axis=1, keepdims=True)
        out = jnp.dot(
            w.astype(jnp.bfloat16), vals[:, window], preferred_element_type=jnp.float32
        )
        out = (acc[:, window] * factor + out) / total
        mixed[:, window] = jnp.where(inside, out, mixed[:, window])
    restyled[...] = (residual[...].astype(jnp.float32) + mixed[...]).astype(jnp.bfloat16)


def call(kernel, outs, ins, scratch=(), flops=0, limit=24):
    moved = sum(a.size * a.dtype.itemsize for a in ins) + sum(
        o.size * o.dtype.itemsize for o in outs
    )
    specs = [SMEM if a.dtype == jnp.int32 else VMEM for a in ins]
    return pl.pallas_call(
        kernel,
        out_shape=list(outs),
        in_specs=specs,
        out_specs=[VMEM] * len(outs),
        scratch_shapes=list(scratch),
        compiler_params=pltpu.CompilerParams(vmem_limit_bytes=limit * 2**20),
        cost_estimate=pl.CostEstimate(flops=flops, bytes_accessed=moved, transcendentals=0),
    )(*ins)


def on_device(latents, gn_gain, conv_weight, conv_bias, ln_gain, qkv_weight):
    _, rows_dev, width, chans = latents.shape
    part = rows_dev * width
    cells = 4 * part
    share = chans // 4
    me = lax.axis_index("rows")
    first = lax.axis_index("tm") == 0
    shape = jax.ShapeDtypeStruct
    bf16, f32 = jnp.bfloat16, jnp.float32
    lat = latents.reshape(part, chans)

    qkv = lax.all_gather(qkv_weight, "rows", axis=0, tiled=True)

    split = lat.reshape(part, 4, share).transpose(1, 0, 2)
    pieces = [lax.dynamic_index_in_dim(split, me ^ flip, 0, keepdims=False) for flip in range(4)]
    blocks = [pieces[0]] + [to_rows(pieces[flip], flip) for flip in (1, 2, 3)]
    gain = lax.dynamic_slice_in_dim(gn_gain, me * share, share).reshape(1, share)
    group = jnp.arange(share) // (chans // GROUPS)
    pool = (group[:, None] == group[None, :]).astype(f32)
    keep, send = call(
        functools.partial(conv_kernel, width),
        [shape((2, part, chans), f32), shape((2, part, chans), bf16)],
        [me.reshape(1), *blocks, gain, conv_weight.reshape(3, 3 * share, chans), pool],
        [
            pltpu.VMEM((cells, share), f32),
            pltpu.VMEM((cells + 2 * width, 3 * share), bf16),
            pltpu.VMEM((cells, chans), f32),
        ],
        flops=2 * cells * 9 * share * chans,
    )
    core = to_rows(send, 1)
    chip = to_rows((keep[1] + core[1].astype(f32)).astype(bf16), 2)
    residual, feats = call(
        norm_kernel,
        [shape((part, chans), bf16)] * 2,
        [lat, keep, core, chip, conv_bias.reshape(1, chans), ln_gain.reshape(1, chans)],
    )

    devices = lax.axis_size("tm")
    prev = lax.ppermute(feats, "tm", [(i, i + 1) for i in range(devices - 1)])
    prev = gathered(jnp.where(first, feats, prev))
    anchor = jnp.where(first, feats, jnp.zeros_like(feats))
    for route in tree_levels(devices):
        anchor = anchor + lax.ppermute(anchor, BOTH, route)
    anchor = gathered(anchor)

    scratch = [
        pltpu.VMEM((cells, chans), bf16),
        pltpu.VMEM((cells, chans), bf16),
        pltpu.VMEM((cells, chans), bf16),
    ]
    flops = 2 * cells * chans * 2 * chans + 4 * part * cells * chans
    query, top, den, acc = call(
        prev_kernel,
        [
            shape((part, chans), bf16),
            shape((part, HEADS), f32),
            shape((part, HEADS), f32),
            shape((part, chans), f32),
        ],
        [feats, *prev, qkv],
        scratch,
        flops=flops,
    )
    (restyled,) = call(
        anchor_kernel,
        [shape((part, chans), bf16)],
        [query, *anchor, qkv, top, den, acc, residual],
        scratch + [pltpu.VMEM((part, chans), f32)],
        flops=flops,
    )
    return restyled.reshape(1, rows_dev, width, chans)


def solution(mesh):
    return jax.shard_map(
        on_device,
        mesh=mesh,
        in_specs=(
            P("tm", "rows", None, None),
            P(),
            P(None, "rows", None),
            P(),
            P(),
            P("rows", None),
        ),
        out_specs=P("tm", "rows", None, None),
        check_vma=False,
    )
```

```python
import functools
import jax
import jax.numpy as jnp
from jax import lax
from jax.experimental import pallas as pl
from jax.experimental.pallas import tpu as pltpu
from jax.sharding import PartitionSpec as P

HEADS = 8
GROUPS = 32
EPS = 1e-05
BOTH = ("tm", "rows")
VMEM = pl.BlockSpec(memory_space=pltpu.VMEM)
SMEM = pl.BlockSpec(memory_space=pltpu.SMEM)


def tree_levels(devices):
    if devices == 128:
        z = [("z", s) for s in (8, 4, 2, 1)]
        x = [("x", s) for s in (2, 1)]
        y = [("y", 1)]
        size = {"y": 2, "z": 16, "x": 4}
        orders = (z + x + y, x + y + z)

        def index(at, sign):
            return (at["y"] * 16 + (sign * at["z"]) % 16) * 4 + at["x"]

    else:
        steps = []
        while 2 ** len(steps) < devices:
            steps.insert(0, ("z", 2 ** len(steps)))
        size = {"z": devices}
        orders = (steps, steps)

        def index(at, sign):
            return at["z"]

    levels = [[] for _ in orders[0]]
    for core, order in enumerate(orders):
        sign = 1 - 2 * core
        known = [{axis: 0 for axis in size}]
        for level, (axis, step) in enumerate(order):
            fresh = []
            for at in known:
                to = dict(at)
                to[axis] = at[axis] + step
                fresh.append(to)
                for chip in range(2):
                    row = chip * 2 + core
                    levels[level].append((index(at, sign) * 4 + row, index(to, sign) * 4 + row))
            known = known + fresh
    return levels


def to_rows(x, flip):
    return lax.ppermute(x, "rows", [(i, i ^ flip) for i in range(4)])


def after(x, *done):
    return lax.optimization_barrier((x, *done))[0]


def gathered(x):
    core = to_rows(x, 1)
    chip = to_rows(x, 2)
    return x, core, chip, to_rows(chip, 1)


def split_kernel(share, me_ref, own, core, mine, away):
    for out, want in ((mine, me_ref[0]), (away, me_ref[0] ^ 2)):
        for block in range(4):

            @pl.when(want == block)
            def _():
                for at, source in enumerate((own, core)):
                    out[at] = source[:, block * share : (block + 1) * share]


def conv_kernel(width, me_ref, mine, came, gain, weight, pool, keep, send, x_ref, taps, acc):
    me = me_ref[0]
    blocks = (mine[0], mine[1], came[0], came[1])
    cells, chans = x_ref.shape
    part = cells // 4
    for flip, block in enumerate(blocks):
        at = pl.multiple_of((me ^ flip) * part, part)
        x_ref[pl.ds(at, part), :] = block.astype(jnp.float32)
    values = x_ref[...]

    def group_mean(column):
        wide = jnp.broadcast_to(column, (8, chans))
        out = jnp.dot(
            wide, pool[...], precision=lax.Precision.HIGHEST, preferred_element_type=jnp.float32
        )
        return out[:1]

    scale = 1.0 / (cells * (640 // GROUPS))
    mean = group_mean(jnp.sum(values, axis=0, keepdims=True)) * scale
    centred = values - mean
    spread = group_mean(jnp.sum(centred * centred, axis=0, keepdims=True)) * scale
    normed = centred * (lax.rsqrt(spread + EPS) * gain[pl.ds(me, 1), :])
    act = normed / (1.0 + jnp.exp(-normed))
    act = act.astype(jnp.bfloat16).astype(jnp.float32)
    column = lax.broadcasted_iota(jnp.int32, (cells, 1), 0) & (width - 1)
    before = jnp.where(column == 0, 0.0, pltpu.roll(act, 1, 0))
    after = jnp.where(column == width - 1, 0.0, pltpu.roll(act, cells - 1, 0))
    taps[:width, :] = jnp.zeros((width, taps.shape[1]), jnp.bfloat16)
    taps[width + cells :, :] = jnp.zeros((width, taps.shape[1]), jnp.bfloat16)
    taps[width : width + cells, :] = jnp.concatenate([before, act, after], axis=1).astype(
        jnp.bfloat16
    )
    acc[...] = sum(
        jnp.dot(
            taps[row * width : row * width + cells, :],
            weight[row],
            preferred_element_type=jnp.float32,
        )
        for row in range(3)
    )
    for flip in range(4):
        at = pl.multiple_of((me ^ flip) * part, part)
        out = acc[pl.ds(at, part), :]
        if flip % 2 == 0:
            keep[flip // 2] = out
        else:
            send[flip // 2] = out.astype(jnp.bfloat16)


def norm_kernel(lat, kept, core, chip, bias, gain, residual, feats):
    conv = kept[0] + core[0].astype(jnp.float32) + chip[...].astype(jnp.float32)
    res = (lat[...].astype(jnp.float32) + conv + bias[...]).astype(jnp.bfloat16)
    residual[...] = res
    rfloat = res.astype(jnp.float32)
    dev = rfloat - jnp.mean(rfloat, axis=1, keepdims=True)
    var = jnp.mean(dev * dev, axis=1, keepdims=True)
    feats[...] = (dev * lax.rsqrt(var + EPS) * gain[...]).astype(jnp.bfloat16)


def head_window(head, head_dim, chans):
    low = head * head_dim // 128 * 128
    high = min(-(-(head + 1) * head_dim // 128) * 128, chans)
    lane = low + lax.broadcasted_iota(jnp.int32, (1, high - low), 1)
    inside = (lane >= head * head_dim) & (lane < (head + 1) * head_dim)
    return slice(low, high), inside


def project(blocks, weight, joined, keys, vals):
    part, chans = blocks[0].shape
    for at, block in enumerate(blocks):
        joined[at * part : (at + 1) * part, :] = block[...]
    for out, first in ((keys, chans), (vals, 2 * chans)):
        out[...] = jnp.dot(
            joined[...], weight[:, first : first + chans], preferred_element_type=jnp.float32
        ).astype(jnp.bfloat16)


def scores_of(query, keys, head, window, inside):
    q_head = jnp.where(inside, query[:, window], 0)
    return lax.dot_general(
        q_head,
        keys[:, window],
        (((1,), (1,)), ((), ())),
        preferred_element_type=jnp.float32,
    )


def prev_kernel(
    me_ref, own, p0, p1, p2, p3, w0, w1, w2, w3, query, top, den, acc, weight, joined, keys, vals
):
    me = me_ref[0]
    part, chans = own.shape
    share = w0.shape[0]
    for flip, shard in enumerate((w0, w1, w2, w3)):
        at = pl.multiple_of((me ^ flip) * share, share)
        weight[pl.ds(at, share), :] = shard[...]
    head_dim = chans // HEADS
    scale = head_dim ** (-0.5)
    query[...] = jnp.dot(
        own[...], weight[:, :chans], preferred_element_type=jnp.float32
    ).astype(jnp.bfloat16)
    project((p0, p1, p2, p3), weight, joined, keys, vals)
    acc[...] = jnp.zeros_like(acc)
    for head in range(HEADS):
        window, inside = head_window(head, head_dim, chans)
        s = scores_of(query, keys, head, window, inside)
        peak = jnp.max(s, axis=1, keepdims=True)
        w = jnp.exp((s - peak) * scale)
        top[:, head : head + 1] = peak
        den[:, head : head + 1] = jnp.sum(w, axis=1, keepdims=True)
        out = jnp.dot(
            w.astype(jnp.bfloat16), vals[:, window], preferred_element_type=jnp.float32
        )
        acc[:, window] = jnp.where(inside, out, acc[:, window])


def anchor_kernel(
    query, a0, a1, a2, a3, weight, top, den, acc, residual, restyled, joined, keys, vals, mixed
):
    part, chans = query.shape
    head_dim = chans // HEADS
    scale = head_dim ** (-0.5)
    project((a0, a1, a2, a3), weight, joined, keys, vals)
    for head in range(HEADS):
        window, inside = head_window(head, head_dim, chans)
        s = scores_of(query, keys, head, window, inside)
        old = top[:, head : head + 1]
        peak = jnp.maximum(old, jnp.max(s, axis=1, keepdims=True))
        factor = jnp.exp((old - peak) * scale)
        w = jnp.exp((s - peak) * scale)
        total = den[:, head : head + 1] * factor + jnp.sum(w, axis=1, keepdims=True)
        out = jnp.dot(
            w.astype(jnp.bfloat16), vals[:, window], preferred_element_type=jnp.float32
        )
        out = (acc[:, window] * factor + out) / total
        mixed[:, window] = jnp.where(inside, out, mixed[:, window])
    restyled[...] = (residual[...].astype(jnp.float32) + mixed[...]).astype(jnp.bfloat16)


def call(kernel, outs, ins, scratch=(), flops=0, limit=24):
    moved = sum(a.size * a.dtype.itemsize for a in ins) + sum(
        o.size * o.dtype.itemsize for o in outs
    )
    specs = [SMEM if a.dtype == jnp.int32 else VMEM for a in ins]
    return pl.pallas_call(
        kernel,
        out_shape=list(outs),
        in_specs=specs,
        out_specs=[VMEM] * len(outs),
        scratch_shapes=list(scratch),
        compiler_params=pltpu.CompilerParams(vmem_limit_bytes=limit * 2**20),
        cost_estimate=pl.CostEstimate(flops=flops, bytes_accessed=moved, transcendentals=0),
    )(*ins)


def on_device(latents, gn_gain, conv_weight, conv_bias, ln_gain, qkv_weight):
    _, rows_dev, width, chans = latents.shape
    part = rows_dev * width
    cells = 4 * part
    share = chans // 4
    me = lax.axis_index("rows")
    first = lax.axis_index("tm") == 0
    shape = jax.ShapeDtypeStruct
    bf16, f32 = jnp.bfloat16, jnp.float32
    lat = latents.reshape(part, chans)

    mine, away = call(
        functools.partial(split_kernel, share),
        [shape((2, part, share), bf16)] * 2,
        [me.reshape(1), lat, to_rows(lat, 1)],
    )
    came = to_rows(away, 2)
    group = jnp.arange(share) // (chans // GROUPS)
    pool = (group[:, None] == group[None, :]).astype(f32)
    keep, send = call(
        functools.partial(conv_kernel, width),
        [shape((2, part, chans), f32), shape((2, part, chans), bf16)],
        [me.reshape(1), mine, came, gn_gain.reshape(4, share), conv_weight.reshape(3, 3 * share, chans), pool],
        [
            pltpu.VMEM((cells, share), f32),
            pltpu.VMEM((cells + 2 * width, 3 * share), bf16),
            pltpu.VMEM((cells, chans), f32),
        ],
        flops=2 * cells * 9 * share * chans,
    )
    core = to_rows(send, 1)
    half = (keep[1] + core[1].astype(f32)).astype(bf16)
    chip = to_rows(half, 2)
    devices = lax.axis_size("tm")
    far = [
        (tm * 4 + row, (tm + devices // 2) % devices * 4 + (row ^ 2))
        for tm in range(devices)
        for row in range(4)
    ]
    weight_chip = lax.ppermute(after(qkv_weight, half), BOTH, far)
    residual, feats = call(
        norm_kernel,
        [shape((part, chans), bf16)] * 2,
        [lat, keep, core, chip, conv_bias.reshape(1, chans), ln_gain.reshape(1, chans)],
    )

    routes = tree_levels(devices)
    tree = lambda level, x: x + lax.ppermute(x, BOTH, routes[level])
    routes = routes + [[]] * (7 - len(routes))
    anchor = tree(0, jnp.where(first, feats, jnp.zeros_like(feats)))
    prev = lax.ppermute(after(feats, anchor), "tm", [(i, i + 1) for i in range(devices - 1)])
    anchor = tree(1, anchor)
    prev = jnp.where(first, feats, prev)
    anchor = after(anchor, prev)
    prev_core = to_rows(prev, 1)
    prev_chip = to_rows(prev, 2)
    anchor = after(tree(2, anchor), prev_core)
    weight_core = to_rows(after(qkv_weight, anchor), 1)
    anchor = after(tree(3, anchor), prev_chip, weight_core)
    prev_last = to_rows(after(prev_chip, anchor), 1)
    weight_last = to_rows(after(weight_chip, anchor), 1)
    anchor = after(tree(4, anchor), prev_last)
    anchor = after(tree(5, anchor), weight_last)
    prev = (prev, prev_core, prev_chip, prev_last)
    qkv = [qkv_weight, weight_core, weight_chip, weight_last]

    scratch = [
        pltpu.VMEM((cells, chans), bf16),
        pltpu.VMEM((cells, chans), bf16),
        pltpu.VMEM((cells, chans), bf16),
    ]
    flops = 2 * cells * chans * 2 * chans + 4 * part * cells * chans
    query, top, den, acc, weight = call(
        prev_kernel,
        [
            shape((part, chans), bf16),
            shape((part, HEADS), f32),
            shape((part, HEADS), f32),
            shape((part, chans), f32),
            shape((chans, 3 * chans), bf16),
        ],
        [me.reshape(1), after(feats, anchor), *prev, *qkv],
        scratch,
        flops=flops,
    )
    anchor = gathered(after(tree(6, anchor), acc))
    (restyled,) = call(
        anchor_kernel,
        [shape((part, chans), bf16)],
        [query, *anchor, weight, top, den, acc, residual],
        scratch + [pltpu.VMEM((part, chans), f32)],
        flops=flops,
    )
    return restyled.reshape(1, rows_dev, width, chans)


def solution(mesh):
    return jax.shard_map(
        on_device,
        mesh=mesh,
        in_specs=(
            P("tm", "rows", None, None),
            P(),
            P(None, "rows", None),
            P(),
            P(),
            P("rows", None),
        ),
        out_specs=P("tm", "rows", None, None),
        check_vma=False,
    )
```

```python
import functools
import jax
import jax.numpy as jnp
from jax import lax
from jax.experimental import pallas as pl
from jax.experimental.pallas import tpu as pltpu
from jax.sharding import PartitionSpec as P

HEADS = 8
GROUPS = 32
EPS = 1e-05
BOTH = ("tm", "rows")
VMEM = pl.BlockSpec(memory_space=pltpu.VMEM)
SMEM = pl.BlockSpec(memory_space=pltpu.SMEM)


def tree_levels(devices):
    if devices == 128:
        z = [("z", s) for s in (8, 4, 2, 1)]
        x = [("x", s) for s in (2, 1)]
        y = [("y", 1)]
        size = {"y": 2, "z": 16, "x": 4}
        orders = (z + x + y, x + y + z)

        def index(at, sign):
            return (at["y"] * 16 + (sign * at["z"]) % 16) * 4 + at["x"]

    else:
        steps = []
        while 2 ** len(steps) < devices:
            steps.insert(0, ("z", 2 ** len(steps)))
        size = {"z": devices}
        orders = (steps, steps)

        def index(at, sign):
            return at["z"]

    levels = [[] for _ in orders[0]]
    for core, order in enumerate(orders):
        sign = 1 - 2 * core
        known = [{axis: 0 for axis in size}]
        for level, (axis, step) in enumerate(order):
            fresh = []
            for at in known:
                to = dict(at)
                to[axis] = at[axis] + step
                fresh.append(to)
                for chip in range(2):
                    row = chip * 2 + core
                    levels[level].append((index(at, sign) * 4 + row, index(to, sign) * 4 + row))
            known = known + fresh
    return levels


def to_rows(x, flip):
    return lax.ppermute(x, "rows", [(i, i ^ flip) for i in range(4)])


def after(x, *done):
    return lax.optimization_barrier((x, *done))[0]


def gathered(x):
    core = to_rows(x, 1)
    chip = to_rows(x, 2)
    return x, core, chip, to_rows(chip, 1)


def split_kernel(share, me_ref, own, core, mine, away):
    for out, want in ((mine, me_ref[0]), (away, me_ref[0] ^ 2)):
        for block in range(4):

            @pl.when(want == block)
            def _():
                for at, source in enumerate((own, core)):
                    out[at] = source[:, block * share : (block + 1) * share]


def conv_kernel(width, me_ref, mine, came, gain, weight, pool, keep, send, x_ref, taps, acc):
    me = me_ref[0]
    blocks = (mine[0], mine[1], came[0], came[1])
    cells, chans = x_ref.shape
    part = cells // 4
    for flip, block in enumerate(blocks):
        at = pl.multiple_of((me ^ flip) * part, part)
        x_ref[pl.ds(at, part), :] = block.astype(jnp.float32)
    values = x_ref[...]

    def group_mean(column):
        wide = jnp.broadcast_to(column, (8, chans))
        out = jnp.dot(
            wide, pool[...], precision=lax.Precision.HIGHEST, preferred_element_type=jnp.float32
        )
        return out[:1]

    scale = 1.0 / (cells * (640 // GROUPS))
    mean = group_mean(jnp.sum(values, axis=0, keepdims=True)) * scale
    centred = values - mean
    spread = group_mean(jnp.sum(centred * centred, axis=0, keepdims=True)) * scale
    normed = centred * (lax.rsqrt(spread + EPS) * gain[pl.ds(me, 1), :])
    act = normed / (1.0 + jnp.exp(-normed))
    act = act.astype(jnp.bfloat16).astype(jnp.float32)
    column = lax.broadcasted_iota(jnp.int32, (cells, 1), 0) & (width - 1)
    before = jnp.where(column == 0, 0.0, pltpu.roll(act, 1, 0))
    after = jnp.where(column == width - 1, 0.0, pltpu.roll(act, cells - 1, 0))
    taps[:width, :] = jnp.zeros((width, taps.shape[1]), jnp.bfloat16)
    taps[width + cells :, :] = jnp.zeros((width, taps.shape[1]), jnp.bfloat16)
    taps[width : width + cells, :] = jnp.concatenate([before, act, after], axis=1).astype(
        jnp.bfloat16
    )
    acc[...] = sum(
        jnp.dot(
            taps[row * width : row * width + cells, :],
            weight[row],
            preferred_element_type=jnp.float32,
        )
        for row in range(3)
    )
    for flip in range(4):
        at = pl.multiple_of((me ^ flip) * part, part)
        out = acc[pl.ds(at, part), :]
        if flip % 2 == 0:
            keep[flip // 2] = out
        else:
            send[flip // 2] = out.astype(jnp.bfloat16)


def norm_kernel(lat, kept, core, chip, bias, gain, residual, feats):
    conv = kept[0] + core[0].astype(jnp.float32) + chip[...].astype(jnp.float32)
    res = (lat[...].astype(jnp.float32) + conv + bias[...]).astype(jnp.bfloat16)
    residual[...] = res
    rfloat = res.astype(jnp.float32)
    dev = rfloat - jnp.mean(rfloat, axis=1, keepdims=True)
    var = jnp.mean(dev * dev, axis=1, keepdims=True)
    feats[...] = (dev * lax.rsqrt(var + EPS) * gain[...]).astype(jnp.bfloat16)


def head_window(head, head_dim, chans):
    low = head * head_dim // 128 * 128
    high = min(-(-(head + 1) * head_dim // 128) * 128, chans)
    lane = low + lax.broadcasted_iota(jnp.int32, (1, high - low), 1)
    inside = (lane >= head * head_dim) & (lane < (head + 1) * head_dim)
    return slice(low, high), inside


def project(blocks, weight, joined, keys, vals):
    part, chans = blocks[0].shape
    for at, block in enumerate(blocks):
        joined[at * part : (at + 1) * part, :] = block[...]
    for out, first in ((keys, chans), (vals, 2 * chans)):
        out[...] = jnp.dot(
            joined[...], weight[:, first : first + chans], preferred_element_type=jnp.float32
        ).astype(jnp.bfloat16)


def scores_of(query, keys, head, window, inside):
    q_head = jnp.where(inside, query[:, window], 0)
    return lax.dot_general(
        q_head,
        keys[:, window],
        (((1,), (1,)), ((), ())),
        preferred_element_type=jnp.float32,
    )


def prev_kernel(
    me_ref, own, p0, p1, p2, p3, w0, w1, w2, w3, query, top, den, acc, weight, joined, keys, vals
):
    me = me_ref[0]
    part, chans = own.shape
    share = w0.shape[0]
    for flip, shard in enumerate((w0, w1, w2, w3)):
        at = pl.multiple_of((me ^ flip) * share, share)
        weight[pl.ds(at, share), :] = shard[...]
    head_dim = chans // HEADS
    scale = head_dim ** (-0.5)
    query[...] = jnp.dot(
        own[...], weight[:, :chans], preferred_element_type=jnp.float32
    ).astype(jnp.bfloat16)
    project((p0, p1, p2, p3), weight, joined, keys, vals)
    acc[...] = jnp.zeros_like(acc)
    for head in range(HEADS):
        window, inside = head_window(head, head_dim, chans)
        s = scores_of(query, keys, head, window, inside)
        peak = jnp.max(s, axis=1, keepdims=True)
        w = jnp.exp((s - peak) * scale)
        top[:, head : head + 1] = peak
        den[:, head : head + 1] = jnp.sum(w, axis=1, keepdims=True)
        out = jnp.dot(
            w.astype(jnp.bfloat16), vals[:, window], preferred_element_type=jnp.float32
        )
        acc[:, window] = jnp.where(inside, out, acc[:, window])


def attend(blocks, query, weight, top, den, acc, joined, keys, vals):
    head_dim = query.shape[1] // HEADS
    scale = head_dim ** (-0.5)
    project(blocks, weight, joined, keys, vals)
    for head in range(HEADS):
        window, inside = head_window(head, head_dim, query.shape[1])
        s = scores_of(query, keys, head, window, inside)
        old = top[:, head : head + 1]
        peak = jnp.maximum(old, jnp.max(s, axis=1, keepdims=True))
        factor = jnp.exp((old - peak) * scale)
        w = jnp.exp((s - peak) * scale)
        total = den[:, head : head + 1] * factor + jnp.sum(w, axis=1, keepdims=True)
        out = jnp.dot(
            w.astype(jnp.bfloat16), vals[:, window], preferred_element_type=jnp.float32
        )
        yield head, window, inside, peak, total, acc[:, window] * factor + out


def more_kernel(
    query, a0, a1, weight, top, den, acc, new_top, new_den, new_acc, joined, keys, vals
):
    for head, window, inside, peak, total, out in attend(
        (a0, a1), query, weight, top, den, acc, joined, keys, vals
    ):
        new_top[:, head : head + 1] = peak
        new_den[:, head : head + 1] = total
        new_acc[:, window] = jnp.where(inside, out, new_acc[:, window])


def last_kernel(
    query, a0, a1, weight, top, den, acc, residual, restyled, joined, keys, vals, mixed
):
    for head, window, inside, _, total, out in attend(
        (a0, a1), query, weight, top, den, acc, joined, keys, vals
    ):
        mixed[:, window] = jnp.where(inside, out / total, mixed[:, window])
    restyled[...] = (residual[...].astype(jnp.float32) + mixed[...]).astype(jnp.bfloat16)


def call(kernel, outs, ins, scratch=(), flops=0, limit=24):
    moved = sum(a.size * a.dtype.itemsize for a in ins) + sum(
        o.size * o.dtype.itemsize for o in outs
    )
    specs = [SMEM if a.dtype == jnp.int32 else VMEM for a in ins]
    return pl.pallas_call(
        kernel,
        out_shape=list(outs),
        in_specs=specs,
        out_specs=[VMEM] * len(outs),
        scratch_shapes=list(scratch),
        compiler_params=pltpu.CompilerParams(vmem_limit_bytes=limit * 2**20),
        cost_estimate=pl.CostEstimate(flops=flops, bytes_accessed=moved, transcendentals=0),
    )(*ins)


def on_device(latents, gn_gain, conv_weight, conv_bias, ln_gain, qkv_weight):
    _, rows_dev, width, chans = latents.shape
    part = rows_dev * width
    cells = 4 * part
    share = chans // 4
    me = lax.axis_index("rows")
    first = lax.axis_index("tm") == 0
    shape = jax.ShapeDtypeStruct
    bf16, f32 = jnp.bfloat16, jnp.float32
    lat = latents.reshape(part, chans)

    mine, away = call(
        functools.partial(split_kernel, share),
        [shape((2, part, share), bf16)] * 2,
        [me.reshape(1), lat, to_rows(lat, 1)],
    )
    devices = lax.axis_size("tm")
    far = [
        (tm * 4 + row, (tm + devices // 2) % devices * 4 + (row ^ 2))
        for tm in range(devices)
        for row in range(4)
    ]
    cut = share // 3 // 16 * 16
    chunk = lambda low, high, *done: lax.ppermute(
        after(qkv_weight[low:high], *done), BOTH, far
    )
    chunk0 = chunk(0, cut, away)
    came = after(to_rows(away, 2), chunk0)
    chunk1 = chunk(cut, 2 * cut, came)
    group = jnp.arange(share) // (chans // GROUPS)
    pool = (group[:, None] == group[None, :]).astype(f32)
    keep, send = call(
        functools.partial(conv_kernel, width),
        [shape((2, part, chans), f32), shape((2, part, chans), bf16)],
        [me.reshape(1), mine, came, gn_gain.reshape(4, share), conv_weight.reshape(3, 3 * share, chans), pool],
        [
            pltpu.VMEM((cells, share), f32),
            pltpu.VMEM((cells + 2 * width, 3 * share), bf16),
            pltpu.VMEM((cells, chans), f32),
        ],
        flops=2 * cells * 9 * share * chans,
    )
    core = to_rows(send, 1)
    half = after((keep[1] + core[1].astype(f32)).astype(bf16), chunk1)
    chip = to_rows(half, 2)
    chunk2 = chunk(2 * cut, share, half)
    chip = after(chip, chunk2)
    residual, feats = call(
        norm_kernel,
        [shape((part, chans), bf16)] * 2,
        [lat, keep, core, chip, conv_bias.reshape(1, chans), ln_gain.reshape(1, chans)],
    )

    routes = tree_levels(devices)
    tree = lambda level, x: x + lax.ppermute(x, BOTH, routes[level])
    routes = routes + [[]] * (7 - len(routes))
    weight_chip = jnp.concatenate([chunk0, chunk1, chunk2], axis=0)
    anchor = tree(0, jnp.where(first, feats, jnp.zeros_like(feats)))
    prev = lax.ppermute(after(feats, anchor), "tm", [(i, i + 1) for i in range(devices - 1)])
    anchor = tree(1, anchor)
    prev = jnp.where(first, feats, prev)
    anchor = after(anchor, prev)
    prev_core = to_rows(prev, 1)
    prev_chip = to_rows(prev, 2)
    anchor = after(tree(2, anchor), prev_core)
    weight_core = to_rows(after(qkv_weight, anchor), 1)
    anchor = after(tree(3, anchor), prev_chip, weight_core)
    prev_last = to_rows(after(prev_chip, anchor), 1)
    anchor = after(tree(4, anchor), prev_last)
    weight_last = to_rows(after(weight_chip, anchor), 1)
    anchor = after(tree(5, anchor), weight_last)
    prev = (prev, prev_core, prev_chip, prev_last)
    qkv = [qkv_weight, weight_core, weight_chip, weight_last]

    scratch = lambda keys: [pltpu.VMEM((keys, chans), bf16)] * 3
    flops = lambda keys: 2 * keys * chans * 2 * chans + 4 * part * keys * chans
    state = [
        shape((part, HEADS), f32),
        shape((part, HEADS), f32),
        shape((part, chans), f32),
    ]
    query, *prior, weight = call(
        prev_kernel,
        [shape((part, chans), bf16), *state, shape((chans, 3 * chans), bf16)],
        [me.reshape(1), after(feats, anchor), *prev, *qkv],
        scratch(cells),
        flops=flops(cells),
    )
    anchor, anchor_core, anchor_chip, anchor_last = gathered(after(tree(6, anchor), prior[2]))
    prior = call(
        more_kernel,
        state,
        [query, anchor, anchor_core, weight, *prior],
        scratch(2 * part),
        flops=flops(2 * part),
    )
    (restyled,) = call(
        last_kernel,
        [shape((part, chans), bf16)],
        [query, anchor_chip, anchor_last, weight, *prior, residual],
        scratch(2 * part) + [pltpu.VMEM((part, chans), f32)],
        flops=flops(2 * part),
    )
    return restyled.reshape(1, rows_dev, width, chans)


def solution(mesh):
    return jax.shard_map(
        on_device,
        mesh=mesh,
        in_specs=(
            P("tm", "rows", None, None),
            P(),
            P(None, "rows", None),
            P(),
            P(),
            P("rows", None),
        ),
        out_specs=P("tm", "rows", None, None),
        check_vma=False,
    )
```

```python
import functools
import jax
import jax.numpy as jnp
from jax import lax
from jax.experimental import pallas as pl
from jax.experimental.pallas import tpu as pltpu
from jax.sharding import PartitionSpec as P

HEADS = 8
GROUPS = 32
EPS = 1e-05
BOTH = ("tm", "rows")
HBM = pl.BlockSpec(memory_space=pltpu.HBM)
VMEM = pl.BlockSpec(memory_space=pltpu.VMEM)
SMEM = pl.BlockSpec(memory_space=pltpu.SMEM)


def tree_levels(devices):
    levels, step = [], devices // 2
    while step:
        levels.append([(tm, tm + step) for tm in range(0, devices, 2 * step)])
        step //= 2
    return levels


def to_rows(x, flip):
    return lax.ppermute(x, "rows", [(i, i ^ flip) for i in range(4)])


def after(x, *done):
    return lax.optimization_barrier((x, *done))[0]


def gathered(x):
    core = to_rows(x, 1)
    chip = to_rows(x, 2)
    return x, core, chip, to_rows(chip, 1)


def split_kernel(share, me_ref, own, core, mine, away):
    for out, want in ((mine, me_ref[0]), (away, me_ref[0] ^ 2)):
        for block in range(4):

            @pl.when(want == block)
            def _():
                for at, source in enumerate((own, core)):
                    out[at] = source[:, block * share : (block + 1) * share]


def conv_kernel(
    width, me_ref, mine, came, gain, weight_hbm, pool, keep, send, x_ref, taps, acc, weight, landed
):
    load = pltpu.make_async_copy(weight_hbm, weight, landed)
    load.start()
    me = me_ref[0]
    blocks = (mine[0], mine[1], came[0], came[1])
    cells, chans = x_ref.shape
    part = cells // 4
    for flip, block in enumerate(blocks):
        at = pl.multiple_of((me ^ flip) * part, part)
        x_ref[pl.ds(at, part), :] = block.astype(jnp.float32)
    values = x_ref[...]

    def group_mean(column):
        wide = jnp.broadcast_to(column, (8, chans))
        out = jnp.dot(
            wide, pool[...], precision=lax.Precision.HIGHEST, preferred_element_type=jnp.float32
        )
        return out[:1]

    scale = 1.0 / (cells * (640 // GROUPS))
    mean = group_mean(jnp.sum(values, axis=0, keepdims=True)) * scale
    centred = values - mean
    spread = group_mean(jnp.sum(centred * centred, axis=0, keepdims=True)) * scale
    normed = centred * (lax.rsqrt(spread + EPS) * gain[pl.ds(me, 1), :])
    act = normed / (1.0 + jnp.exp(-normed))
    act = act.astype(jnp.bfloat16).astype(jnp.float32)
    column = lax.broadcasted_iota(jnp.int32, (cells, 1), 0) & (width - 1)
    before = jnp.where(column == 0, 0.0, pltpu.roll(act, 1, 0))
    after = jnp.where(column == width - 1, 0.0, pltpu.roll(act, cells - 1, 0))
    taps[:width, :] = jnp.zeros((width, taps.shape[1]), jnp.bfloat16)
    taps[width + cells :, :] = jnp.zeros((width, taps.shape[1]), jnp.bfloat16)
    taps[width : width + cells, :] = jnp.concatenate([before, act, after], axis=1).astype(
        jnp.bfloat16
    )
    load.wait()
    acc[...] = sum(
        jnp.dot(
            taps[row * width : row * width + cells, :],
            weight[row],
            preferred_element_type=jnp.float32,
        )
        for row in range(3)
    )
    for flip in range(4):
        at = pl.multiple_of((me ^ flip) * part, part)
        out = acc[pl.ds(at, part), :]
        if flip % 2 == 0:
            keep[flip // 2] = out
        else:
            send[flip // 2] = out.astype(jnp.bfloat16)


def norm_kernel(lat, kept, core, chip, bias, gain, residual, feats):
    conv = kept[0] + core[0].astype(jnp.float32) + chip[...].astype(jnp.float32)
    res = (lat[...].astype(jnp.float32) + conv + bias[...]).astype(jnp.bfloat16)
    residual[...] = res
    rfloat = res.astype(jnp.float32)
    dev = rfloat - jnp.mean(rfloat, axis=1, keepdims=True)
    var = jnp.mean(dev * dev, axis=1, keepdims=True)
    feats[...] = (dev * lax.rsqrt(var + EPS) * gain[...]).astype(jnp.bfloat16)


def head_window(head, head_dim, chans):
    low = head * head_dim // 128 * 128
    high = min(-(-(head + 1) * head_dim // 128) * 128, chans)
    lane = low + lax.broadcasted_iota(jnp.int32, (1, high - low), 1)
    inside = (lane >= head * head_dim) & (lane < (head + 1) * head_dim)
    return slice(low, high), inside


def project(blocks, weight, joined, keys, vals):
    part, chans = blocks[0].shape
    for at, block in enumerate(blocks):
        joined[at * part : (at + 1) * part, :] = block[...]
    for out, first in ((keys, chans), (vals, 2 * chans)):
        out[...] = jnp.dot(
            joined[...], weight[:, first : first + chans], preferred_element_type=jnp.float32
        ).astype(jnp.bfloat16)


def scores_of(query, keys, head, window, inside):
    q_head = jnp.where(inside, query[:, window], 0)
    return lax.dot_general(
        q_head,
        keys[:, window],
        (((1,), (1,)), ((), ())),
        preferred_element_type=jnp.float32,
    )


def prev_kernel(
    me_ref, own, p0, p1, p2, p3, w0, w1, w2, w3, query, top, den, acc, weight, joined, keys, vals
):
    me = me_ref[0]
    part, chans = own.shape
    share = w0.shape[0]
    for flip, shard in enumerate((w0, w1, w2, w3)):
        at = pl.multiple_of((me ^ flip) * share, share)
        weight[pl.ds(at, share), :] = shard[...]
    head_dim = chans // HEADS
    scale = head_dim ** (-0.5)
    query[...] = jnp.dot(
        own[...], weight[:, :chans], preferred_element_type=jnp.float32
    ).astype(jnp.bfloat16)
    project((p0, p1, p2, p3), weight, joined, keys, vals)
    acc[...] = jnp.zeros_like(acc)
    for head in range(HEADS):
        window, inside = head_window(head, head_dim, chans)
        s = scores_of(query, keys, head, window, inside)
        peak = jnp.max(s, axis=1, keepdims=True)
        w = jnp.exp((s - peak) * scale)
        top[:, head : head + 1] = peak
        den[:, head : head + 1] = jnp.sum(w, axis=1, keepdims=True)
        out = jnp.dot(
            w.astype(jnp.bfloat16), vals[:, window], preferred_element_type=jnp.float32
        )
        acc[:, window] = jnp.where(inside, out, acc[:, window])


def attend(blocks, query, weight, top, den, acc, joined, keys, vals):
    head_dim = query.shape[1] // HEADS
    scale = head_dim ** (-0.5)
    project(blocks, weight, joined, keys, vals)
    for head in range(HEADS):
        window, inside = head_window(head, head_dim, query.shape[1])
        s = scores_of(query, keys, head, window, inside)
        old = top[:, head : head + 1]
        peak = jnp.maximum(old, jnp.max(s, axis=1, keepdims=True))
        factor = jnp.exp((old - peak) * scale)
        w = jnp.exp((s - peak) * scale)
        total = den[:, head : head + 1] * factor + jnp.sum(w, axis=1, keepdims=True)
        out = jnp.dot(
            w.astype(jnp.bfloat16), vals[:, window], preferred_element_type=jnp.float32
        )
        yield head, window, inside, peak, total, acc[:, window] * factor + out


def more_kernel(
    query, a0, a1, weight, top, den, acc, new_top, new_den, new_acc, joined, keys, vals
):
    for head, window, inside, peak, total, out in attend(
        (a0, a1), query, weight, top, den, acc, joined, keys, vals
    ):
        new_top[:, head : head + 1] = peak
        new_den[:, head : head + 1] = total
        new_acc[:, window] = jnp.where(inside, out, new_acc[:, window])


def last_kernel(
    query, a0, a1, weight, top, den, acc, residual, restyled, joined, keys, vals, mixed
):
    for head, window, inside, _, total, out in attend(
        (a0, a1), query, weight, top, den, acc, joined, keys, vals
    ):
        mixed[:, window] = jnp.where(inside, out / total, mixed[:, window])
    restyled[...] = (residual[...].astype(jnp.float32) + mixed[...]).astype(jnp.bfloat16)


def call(kernel, outs, ins, scratch=(), flops=0, limit=24, hbm=()):
    moved = sum(a.size * a.dtype.itemsize for a in ins) + sum(
        o.size * o.dtype.itemsize for o in outs
    )
    specs = [
        HBM if i in hbm else SMEM if a.dtype == jnp.int32 else VMEM for i, a in enumerate(ins)
    ]
    return pl.pallas_call(
        kernel,
        out_shape=list(outs),
        in_specs=specs,
        out_specs=[VMEM] * len(outs),
        scratch_shapes=list(scratch),
        compiler_params=pltpu.CompilerParams(vmem_limit_bytes=limit * 2**20),
        cost_estimate=pl.CostEstimate(flops=flops, bytes_accessed=moved, transcendentals=0),
    )(*ins)


def on_device(latents, gn_gain, conv_weight, conv_bias, ln_gain, qkv_weight):
    _, rows_dev, width, chans = latents.shape
    part = rows_dev * width
    cells = 4 * part
    share = chans // 4
    me = lax.axis_index("rows")
    first = lax.axis_index("tm") == 0
    shape = jax.ShapeDtypeStruct
    bf16, f32 = jnp.bfloat16, jnp.float32
    lat = latents.reshape(part, chans)

    mine, away = call(
        functools.partial(split_kernel, share),
        [shape((2, part, share), bf16)] * 2,
        [me.reshape(1), lat, to_rows(lat, 1)],
    )
    came = to_rows(away, 2)
    group = jnp.arange(share) // (chans // GROUPS)
    pool = (group[:, None] == group[None, :]).astype(f32)
    keep, send = call(
        functools.partial(conv_kernel, width),
        [shape((2, part, chans), f32), shape((2, part, chans), bf16)],
        [me.reshape(1), mine, came, gn_gain.reshape(4, share), conv_weight.reshape(3, 3 * share, chans), pool],
        [
            pltpu.VMEM((cells, share), f32),
            pltpu.VMEM((cells + 2 * width, 3 * share), bf16),
            pltpu.VMEM((cells, chans), f32),
            pltpu.VMEM((3, 3 * share, chans), bf16),
            pltpu.SemaphoreType.DMA,
        ],
        hbm=(4,),
        flops=2 * cells * 9 * share * chans,
    )
    core = to_rows(send, 1)
    half = (keep[1] + core[1].astype(f32)).astype(bf16)
    chip = to_rows(half, 2)
    residual, feats = call(
        norm_kernel,
        [shape((part, chans), bf16)] * 2,
        [lat, keep, core, chip, conv_bias.reshape(1, chans), ln_gain.reshape(1, chans)],
    )

    devices = lax.axis_size("tm")
    far = [
        (tm * 4 + row, (tm + devices // 2) % devices * 4 + (row ^ 2))
        for tm in range(devices)
        for row in range(4)
    ]
    cut = share // 3 // 16 * 16
    chunk = lambda low, high, done: lax.ppermute(after(qkv_weight[low:high], done), BOTH, far)
    routes = tree_levels(devices)
    routes = routes + [[]] * (7 - len(routes))
    tree = lambda level, x: x + lax.ppermute(x, "tm", routes[level])
    anchor = tree(0, jnp.where(first, feats, jnp.zeros_like(feats)))
    prev = lax.ppermute(after(feats, anchor), "tm", [(i, i + 1) for i in range(devices - 1)])
    chunk0 = chunk(0, cut, anchor)
    anchor = tree(1, anchor)
    prev = jnp.where(first, feats, prev)
    anchor = after(anchor, prev, chunk0)
    chunk1 = chunk(cut, 2 * cut, anchor)
    prev_core = to_rows(after(prev, anchor), 1)
    anchor = after(tree(2, anchor), prev_core, chunk1)
    chunk2 = chunk(2 * cut, share, anchor)
    weight_core = to_rows(after(qkv_weight, anchor), 1)
    anchor = after(tree(3, anchor), weight_core, chunk2)
    prev_chip = to_rows(after(prev, anchor), 2)
    weight_chip = jnp.concatenate([chunk0, chunk1, chunk2], axis=0)
    weight_last = to_rows(after(weight_chip, anchor), 1)
    anchor = after(tree(4, anchor), prev_chip, weight_last)
    prev_last = to_rows(after(prev_chip, anchor), 1)
    anchor = after(tree(5, anchor), prev_last)
    prev = (prev, prev_core, prev_chip, prev_last)
    qkv = [qkv_weight, weight_core, weight_chip, weight_last]

    scratch = lambda keys: [pltpu.VMEM((keys, chans), bf16)] * 3
    flops = lambda keys: 2 * keys * chans * 2 * chans + 4 * part * keys * chans
    state = [
        shape((part, HEADS), f32),
        shape((part, HEADS), f32),
        shape((part, chans), f32),
    ]
    query, *prior, weight = call(
        prev_kernel,
        [shape((part, chans), bf16), *state, shape((chans, 3 * chans), bf16)],
        [me.reshape(1), after(feats, anchor), *prev, *qkv],
        scratch(cells),
        flops=flops(cells),
    )
    anchor, anchor_core, anchor_chip, anchor_last = gathered(after(tree(6, anchor), prior[2]))
    prior = call(
        more_kernel,
        state,
        [query, anchor, anchor_core, weight, *prior],
        scratch(2 * part),
        flops=flops(2 * part),
    )
    (restyled,) = call(
        last_kernel,
        [shape((part, chans), bf16)],
        [query, anchor_chip, anchor_last, weight, *prior, residual],
        scratch(2 * part) + [pltpu.VMEM((part, chans), f32)],
        flops=flops(2 * part),
    )
    return restyled.reshape(1, rows_dev, width, chans)


def solution(mesh):
    return jax.shard_map(
        on_device,
        mesh=mesh,
        in_specs=(
            P("tm", "rows", None, None),
            P(),
            P(None, "rows", None),
            P(),
            P(),
            P("rows", None),
        ),
        out_specs=P("tm", "rows", None, None),
        check_vma=False,
    )
```

```python
import functools
import jax
import jax.numpy as jnp
from jax import lax
from jax.experimental import pallas as pl
from jax.experimental.pallas import tpu as pltpu
from jax.sharding import PartitionSpec as P

HEADS = 8
GROUPS = 32
EPS = 1e-05
HBM = pl.BlockSpec(memory_space=pltpu.HBM)
VMEM = pl.BlockSpec(memory_space=pltpu.VMEM)
SMEM = pl.BlockSpec(memory_space=pltpu.SMEM)


def tree_levels(devices):
    levels, step = [], devices // 2
    while step:
        levels.append([(tm, tm + step) for tm in range(0, devices, 2 * step)])
        step //= 2
    return levels


def to_rows(x, flip):
    return lax.ppermute(x, "rows", [(i, i ^ flip) for i in range(4)])


def after(x, *done):
    return lax.optimization_barrier((x, *done))[0]


def gathered(x):
    core = to_rows(x, 1)
    chip = to_rows(x, 2)
    return x, core, chip, to_rows(chip, 1)


def fetch_kernel(source, out, landed):
    load = pltpu.make_async_copy(source, out, landed)
    load.start()
    load.wait()


def split_kernel(share, me_ref, own, core, mine, away):
    for out, want in ((mine, me_ref[0]), (away, me_ref[0] ^ 2)):
        for block in range(4):

            @pl.when(want == block)
            def _():
                for at, source in enumerate((own, core)):
                    out[at] = source[:, block * share : (block + 1) * share]


def conv_kernel(
    width, me_ref, mine, came, gain, weight, pool, keep, send, x_ref, taps, acc
):
    me = me_ref[0]
    blocks = (mine[0], mine[1], came[0], came[1])
    cells, chans = x_ref.shape
    part = cells // 4
    for flip, block in enumerate(blocks):
        at = pl.multiple_of((me ^ flip) * part, part)
        x_ref[pl.ds(at, part), :] = block.astype(jnp.float32)
    values = x_ref[...]

    def group_mean(column):
        wide = jnp.broadcast_to(column, (8, chans))
        out = jnp.dot(
            wide, pool[...], precision=lax.Precision.HIGHEST, preferred_element_type=jnp.float32
        )
        return out[:1]

    scale = 1.0 / (cells * (640 // GROUPS))
    mean = group_mean(jnp.sum(values, axis=0, keepdims=True)) * scale
    centred = values - mean
    spread = group_mean(jnp.sum(centred * centred, axis=0, keepdims=True)) * scale
    normed = centred * (lax.rsqrt(spread + EPS) * gain[pl.ds(me, 1), :])
    act = normed / (1.0 + jnp.exp(-normed))
    act = act.astype(jnp.bfloat16).astype(jnp.float32)
    column = lax.broadcasted_iota(jnp.int32, (cells, 1), 0) & (width - 1)
    before = jnp.where(column == 0, 0.0, pltpu.roll(act, 1, 0))
    after = jnp.where(column == width - 1, 0.0, pltpu.roll(act, cells - 1, 0))
    taps[:width, :] = jnp.zeros((width, taps.shape[1]), jnp.bfloat16)
    taps[width + cells :, :] = jnp.zeros((width, taps.shape[1]), jnp.bfloat16)
    taps[width : width + cells, :] = jnp.concatenate([before, act, after], axis=1).astype(
        jnp.bfloat16
    )
    acc[...] = sum(
        jnp.dot(
            taps[row * width : row * width + cells, :],
            weight[row],
            preferred_element_type=jnp.float32,
        )
        for row in range(3)
    )
    for flip in range(4):
        at = pl.multiple_of((me ^ flip) * part, part)
        out = acc[pl.ds(at, part), :]
        if flip % 2 == 0:
            keep[flip // 2] = out
        else:
            send[flip // 2] = out.astype(jnp.bfloat16)


def norm_kernel(lat, kept, core, chip, bias, gain, residual, feats):
    conv = kept[0] + core[0].astype(jnp.float32) + chip[...].astype(jnp.float32)
    res = (lat[...].astype(jnp.float32) + conv + bias[...]).astype(jnp.bfloat16)
    residual[...] = res
    rfloat = res.astype(jnp.float32)
    dev = rfloat - jnp.mean(rfloat, axis=1, keepdims=True)
    var = jnp.mean(dev * dev, axis=1, keepdims=True)
    feats[...] = (dev * lax.rsqrt(var + EPS) * gain[...]).astype(jnp.bfloat16)


def head_window(head, head_dim, chans):
    low = head * head_dim // 128 * 128
    high = min(-(-(head + 1) * head_dim // 128) * 128, chans)
    lane = low + lax.broadcasted_iota(jnp.int32, (1, high - low), 1)
    inside = (lane >= head * head_dim) & (lane < (head + 1) * head_dim)
    return slice(low, high), inside


def project(blocks, weight, joined, keys, vals):
    part, chans = blocks[0].shape
    for at, block in enumerate(blocks):
        joined[at * part : (at + 1) * part, :] = block[...]
    for out, first in ((keys, chans), (vals, 2 * chans)):
        out[...] = jnp.dot(
            joined[...], weight[:, first : first + chans], preferred_element_type=jnp.float32
        ).astype(jnp.bfloat16)


def scores_of(query, keys, head, window, inside):
    q_head = jnp.where(inside, query[:, window], 0)
    return lax.dot_general(
        q_head,
        keys[:, window],
        (((1,), (1,)), ((), ())),
        preferred_element_type=jnp.float32,
    )


def prev_kernel(
    me_ref, own, p0, p1, p2, p3, w0, w1, w2, w3, query, top, den, acc, weight, joined, keys, vals
):
    me = me_ref[0]
    part, chans = own.shape
    share = w0.shape[0]
    for flip, shard in enumerate((w0, w1, w2, w3)):
        at = pl.multiple_of((me ^ flip) * share, share)
        weight[pl.ds(at, share), :] = shard[...]
    head_dim = chans // HEADS
    scale = head_dim ** (-0.5)
    query[...] = jnp.dot(
        own[...], weight[:, :chans], preferred_element_type=jnp.float32
    ).astype(jnp.bfloat16)
    project((p0, p1, p2, p3), weight, joined, keys, vals)
    acc[...] = jnp.zeros_like(acc)
    for head in range(HEADS):
        window, inside = head_window(head, head_dim, chans)
        s = scores_of(query, keys, head, window, inside)
        peak = jnp.max(s, axis=1, keepdims=True)
        w = jnp.exp((s - peak) * scale)
        top[:, head : head + 1] = peak
        den[:, head : head + 1] = jnp.sum(w, axis=1, keepdims=True)
        out = jnp.dot(
            w.astype(jnp.bfloat16), vals[:, window], preferred_element_type=jnp.float32
        )
        acc[:, window] = jnp.where(inside, out, acc[:, window])


def attend(blocks, query, weight, top, den, acc, joined, keys, vals):
    head_dim = query.shape[1] // HEADS
    scale = head_dim ** (-0.5)
    project(blocks, weight, joined, keys, vals)
    for head in range(HEADS):
        window, inside = head_window(head, head_dim, query.shape[1])
        s = scores_of(query, keys, head, window, inside)
        old = top[:, head : head + 1]
        peak = jnp.maximum(old, jnp.max(s, axis=1, keepdims=True))
        factor = jnp.exp((old - peak) * scale)
        w = jnp.exp((s - peak) * scale)
        total = den[:, head : head + 1] * factor + jnp.sum(w, axis=1, keepdims=True)
        out = jnp.dot(
            w.astype(jnp.bfloat16), vals[:, window], preferred_element_type=jnp.float32
        )
        yield head, window, inside, peak, total, acc[:, window] * factor + out


def more_kernel(
    query, a0, a1, weight, top, den, acc, new_top, new_den, new_acc, joined, keys, vals
):
    for head, window, inside, peak, total, out in attend(
        (a0, a1), query, weight, top, den, acc, joined, keys, vals
    ):
        new_top[:, head : head + 1] = peak
        new_den[:, head : head + 1] = total
        new_acc[:, window] = jnp.where(inside, out, new_acc[:, window])


def last_kernel(
    query, a0, a1, weight, top, den, acc, residual, restyled, joined, keys, vals, mixed
):
    for head, window, inside, _, total, out in attend(
        (a0, a1), query, weight, top, den, acc, joined, keys, vals
    ):
        mixed[:, window] = jnp.where(inside, out / total, mixed[:, window])
    restyled[...] = (residual[...].astype(jnp.float32) + mixed[...]).astype(jnp.bfloat16)


def call(kernel, outs, ins, scratch=(), flops=0, limit=24, hbm=()):
    moved = sum(a.size * a.dtype.itemsize for a in ins) + sum(
        o.size * o.dtype.itemsize for o in outs
    )
    specs = [
        HBM if i in hbm else SMEM if a.dtype == jnp.int32 else VMEM for i, a in enumerate(ins)
    ]
    return pl.pallas_call(
        kernel,
        out_shape=list(outs),
        in_specs=specs,
        out_specs=[VMEM] * len(outs),
        scratch_shapes=list(scratch),
        compiler_params=pltpu.CompilerParams(vmem_limit_bytes=limit * 2**20),
        cost_estimate=pl.CostEstimate(flops=flops, bytes_accessed=moved, transcendentals=0),
    )(*ins)


def on_device(latents, gn_gain, conv_weight, conv_bias, ln_gain, qkv_weight):
    _, rows_dev, width, chans = latents.shape
    part = rows_dev * width
    cells = 4 * part
    share = chans // 4
    me = lax.axis_index("rows")
    first = lax.axis_index("tm") == 0
    shape = jax.ShapeDtypeStruct
    bf16, f32 = jnp.bfloat16, jnp.float32
    lat = latents.reshape(part, chans)

    fetched = lambda x: call(
        fetch_kernel, [shape(x.shape, x.dtype)], [x], [pltpu.SemaphoreType.DMA], hbm=(0,)
    )[0]
    lat_core = to_rows(lat, 1)
    lat = fetched(lat)
    mine, away = call(
        functools.partial(split_kernel, share),
        [shape((2, part, share), bf16)] * 2,
        [me.reshape(1), lat, lat_core],
    )
    came = to_rows(away, 2)
    weight_core = to_rows(after(qkv_weight, away), 1)
    taps_weight = fetched(after(conv_weight.reshape(3, 3 * share, chans), away))
    came = after(came, weight_core, taps_weight)
    group = jnp.arange(share) // (chans // GROUPS)
    pool = (group[:, None] == group[None, :]).astype(f32)
    keep, send = call(
        functools.partial(conv_kernel, width),
        [shape((2, part, chans), f32), shape((2, part, chans), bf16)],
        [me.reshape(1), mine, came, gn_gain.reshape(4, share), taps_weight, pool],
        [
            pltpu.VMEM((cells, share), f32),
            pltpu.VMEM((cells + 2 * width, 3 * share), bf16),
            pltpu.VMEM((cells, chans), f32),
        ],
        flops=2 * cells * 9 * share * chans,
    )
    core = to_rows(send, 1)
    half = (keep[1] + core[1].astype(f32)).astype(bf16)
    chip = to_rows(half, 2)
    residual, feats = call(
        norm_kernel,
        [shape((part, chans), bf16)] * 2,
        [lat, keep, core, chip, conv_bias.reshape(1, chans), ln_gain.reshape(1, chans)],
    )

    devices = lax.axis_size("tm")
    routes = tree_levels(devices)
    routes = routes + [[]] * (7 - len(routes))
    tree = lambda level, x: x + lax.ppermute(x, "tm", routes[level])
    cut = share // 4
    chunk = lambda at, done: to_rows(after(qkv_weight[at * cut : (at + 1) * cut], done), 2)
    prev = lax.ppermute(feats, "tm", [(i, i + 1) for i in range(devices - 1)])
    chunks = [chunk(0, feats)]
    anchor = tree(0, jnp.where(first, feats, jnp.zeros_like(feats)))
    prev = jnp.where(first, feats, after(prev, anchor))
    anchor = after(anchor, prev, chunks[0])
    for level in (1, 2, 3):
        chunks.append(chunk(level, anchor))
        anchor = after(tree(level, anchor), chunks[level])
    weight_chip = jnp.concatenate(chunks, axis=0)
    prev_chip = to_rows(after(prev, anchor), 2)
    weight_last = to_rows(after(weight_chip, anchor), 1)
    anchor = after(tree(4, anchor), prev_chip, weight_last)
    prev_core = to_rows(after(prev, anchor), 1)
    prev_last = to_rows(after(prev_chip, anchor), 1)
    anchor = after(tree(5, anchor), prev_core, prev_last)
    prev = (prev, prev_core, prev_chip, prev_last)
    qkv = [qkv_weight, weight_core, weight_chip, weight_last]

    scratch = lambda keys: [pltpu.VMEM((keys, chans), bf16)] * 3
    flops = lambda keys: 2 * keys * chans * 2 * chans + 4 * part * keys * chans
    state = [
        shape((part, HEADS), f32),
        shape((part, HEADS), f32),
        shape((part, chans), f32),
    ]
    query, *prior, weight = call(
        prev_kernel,
        [shape((part, chans), bf16), *state, shape((chans, 3 * chans), bf16)],
        [me.reshape(1), after(feats, anchor), *prev, *qkv],
        scratch(cells),
        flops=flops(cells),
    )
    anchor, anchor_core, anchor_chip, anchor_last = gathered(after(tree(6, anchor), prior[2]))
    prior = call(
        more_kernel,
        state,
        [query, anchor, anchor_core, weight, *prior],
        scratch(2 * part),
        flops=flops(2 * part),
    )
    (restyled,) = call(
        last_kernel,
        [shape((part, chans), bf16)],
        [query, anchor_chip, anchor_last, weight, *prior, residual],
        scratch(2 * part) + [pltpu.VMEM((part, chans), f32)],
        flops=flops(2 * part),
    )
    return restyled.reshape(1, rows_dev, width, chans)


def solution(mesh):
    return jax.shard_map(
        on_device,
        mesh=mesh,
        in_specs=(
            P("tm", "rows", None, None),
            P(),
            P(None, "rows", None),
            P(),
            P(),
            P("rows", None),
        ),
        out_specs=P("tm", "rows", None, None),
        check_vma=False,
    )
```

```python
import functools
import jax
import jax.numpy as jnp
from jax import lax
from jax.experimental import pallas as pl
from jax.experimental.pallas import tpu as pltpu
from jax.sharding import PartitionSpec as P

HEADS = 8
GROUPS = 32
EPS = 1e-05
HBM = pl.BlockSpec(memory_space=pltpu.HBM)
VMEM = pl.BlockSpec(memory_space=pltpu.VMEM)
SMEM = pl.BlockSpec(memory_space=pltpu.SMEM)


def tree_levels(devices):
    levels, step = [], devices // 2
    while step:
        levels.append([(tm, tm + step) for tm in range(0, devices, 2 * step)])
        step //= 2
    return levels


def to_rows(x, flip):
    return lax.ppermute(x, "rows", [(i, i ^ flip) for i in range(4)])


def after(x, *done):
    return lax.optimization_barrier((x, *done))[0]


def fetch_kernel(source, out, landed):
    load = pltpu.make_async_copy(source, out, landed)
    load.start()
    load.wait()


def split_kernel(share, me_ref, own, core, mine, away):
    for out, want in ((mine, me_ref[0]), (away, me_ref[0] ^ 2)):
        for block in range(4):

            @pl.when(want == block)
            def _():
                for at, source in enumerate((own, core)):
                    out[at] = source[:, block * share : (block + 1) * share]


def conv_kernel(
    width, me_ref, mine, came, gain, weight, pool, keep, send, x_ref, taps, acc
):
    me = me_ref[0]
    blocks = (mine[0], mine[1], came[0], came[1])
    cells, chans = x_ref.shape
    part = cells // 4
    for flip, block in enumerate(blocks):
        at = pl.multiple_of((me ^ flip) * part, part)
        x_ref[pl.ds(at, part), :] = block.astype(jnp.float32)
    values = x_ref[...]

    def group_mean(column):
        wide = jnp.broadcast_to(column, (8, chans))
        out = jnp.dot(
            wide, pool[...], precision=lax.Precision.HIGHEST, preferred_element_type=jnp.float32
        )
        return out[:1]

    scale = 1.0 / (cells * (640 // GROUPS))
    mean = group_mean(jnp.sum(values, axis=0, keepdims=True)) * scale
    centred = values - mean
    spread = group_mean(jnp.sum(centred * centred, axis=0, keepdims=True)) * scale
    normed = centred * (lax.rsqrt(spread + EPS) * gain[pl.ds(me, 1), :])
    act = normed / (1.0 + jnp.exp(-normed))
    act = act.astype(jnp.bfloat16).astype(jnp.float32)
    column = lax.broadcasted_iota(jnp.int32, (cells, 1), 0) & (width - 1)
    before = jnp.where(column == 0, 0.0, pltpu.roll(act, 1, 0))
    after = jnp.where(column == width - 1, 0.0, pltpu.roll(act, cells - 1, 0))
    taps[:width, :] = jnp.zeros((width, taps.shape[1]), jnp.bfloat16)
    taps[width + cells :, :] = jnp.zeros((width, taps.shape[1]), jnp.bfloat16)
    taps[width : width + cells, :] = jnp.concatenate([before, act, after], axis=1).astype(
        jnp.bfloat16
    )
    acc[...] = sum(
        jnp.dot(
            taps[row * width : row * width + cells, :],
            weight[row],
            preferred_element_type=jnp.float32,
        )
        for row in range(3)
    )
    for flip in range(4):
        at = pl.multiple_of((me ^ flip) * part, part)
        out = acc[pl.ds(at, part), :]
        if flip % 2 == 0:
            keep[flip // 2] = out
        else:
            send[flip // 2] = out.astype(jnp.bfloat16)


def norm_kernel(lat, kept, core, chip, bias, gain, residual, feats):
    conv = kept[0] + core[0].astype(jnp.float32) + chip[...].astype(jnp.float32)
    res = (lat[...].astype(jnp.float32) + conv + bias[...]).astype(jnp.bfloat16)
    residual[...] = res
    rfloat = res.astype(jnp.float32)
    dev = rfloat - jnp.mean(rfloat, axis=1, keepdims=True)
    var = jnp.mean(dev * dev, axis=1, keepdims=True)
    feats[...] = (dev * lax.rsqrt(var + EPS) * gain[...]).astype(jnp.bfloat16)


def head_window(head, head_dim, chans):
    low = head * head_dim // 128 * 128
    high = min(-(-(head + 1) * head_dim // 128) * 128, chans)
    lane = low + lax.broadcasted_iota(jnp.int32, (1, high - low), 1)
    inside = (lane >= head * head_dim) & (lane < (head + 1) * head_dim)
    return slice(low, high), inside


def project(blocks, weight, joined, keys, vals):
    part, chans = blocks[0].shape
    for at, block in enumerate(blocks):
        joined[at * part : (at + 1) * part, :] = block[...]
    for out, first in ((keys, chans), (vals, 2 * chans)):
        out[...] = jnp.dot(
            joined[...], weight[:, first : first + chans], preferred_element_type=jnp.float32
        ).astype(jnp.bfloat16)


def scores_of(query, keys, head, window, inside):
    q_head = jnp.where(inside, query[:, window], 0)
    return lax.dot_general(
        q_head,
        keys[:, window],
        (((1,), (1,)), ((), ())),
        preferred_element_type=jnp.float32,
    )


def first_kernel(feats, a0, a1, weight, query, top, den, acc, joined, keys, vals):
    chans = feats.shape[1]
    head_dim = chans // HEADS
    scale = head_dim ** (-0.5)
    query[...] = jnp.dot(
        feats[...], weight[:, :chans], preferred_element_type=jnp.float32
    ).astype(jnp.bfloat16)
    project((a0, a1), weight, joined, keys, vals)
    for head in range(HEADS):
        window, inside = head_window(head, head_dim, chans)
        s = scores_of(query, keys, head, window, inside)
        peak = jnp.max(s, axis=1, keepdims=True)
        w = jnp.exp((s - peak) * scale)
        top[:, head : head + 1] = peak
        den[:, head : head + 1] = jnp.sum(w, axis=1, keepdims=True)
        out = jnp.dot(
            w.astype(jnp.bfloat16), vals[:, window], preferred_element_type=jnp.float32
        )
        acc[:, window] = jnp.where(inside, out, acc[:, window])


def attend(blocks, query, weight, top, den, acc, joined, keys, vals):
    head_dim = query.shape[1] // HEADS
    scale = head_dim ** (-0.5)
    project(blocks, weight, joined, keys, vals)
    for head in range(HEADS):
        window, inside = head_window(head, head_dim, query.shape[1])
        s = scores_of(query, keys, head, window, inside)
        old = top[:, head : head + 1]
        peak = jnp.maximum(old, jnp.max(s, axis=1, keepdims=True))
        factor = jnp.exp((old - peak) * scale)
        w = jnp.exp((s - peak) * scale)
        total = den[:, head : head + 1] * factor + jnp.sum(w, axis=1, keepdims=True)
        out = jnp.dot(
            w.astype(jnp.bfloat16), vals[:, window], preferred_element_type=jnp.float32
        )
        yield head, window, inside, peak, total, acc[:, window] * factor + out


def more_kernel(
    query, a0, weight, top, den, acc, new_top, new_den, new_acc, joined, keys, vals
):
    for head, window, inside, peak, total, out in attend(
        (a0,), query, weight, top, den, acc, joined, keys, vals
    ):
        new_top[:, head : head + 1] = peak
        new_den[:, head : head + 1] = total
        new_acc[:, window] = jnp.where(inside, out, new_acc[:, window])


def last_kernel(
    query, a0, weight, top, den, acc, residual, restyled, joined, keys, vals, mixed
):
    for head, window, inside, _, total, out in attend(
        (a0,), query, weight, top, den, acc, joined, keys, vals
    ):
        mixed[:, window] = jnp.where(inside, out / total, mixed[:, window])
    restyled[...] = (residual[...].astype(jnp.float32) + mixed[...]).astype(jnp.bfloat16)


def call(kernel, outs, ins, scratch=(), flops=0, limit=24, hbm=()):
    moved = sum(a.size * a.dtype.itemsize for a in ins) + sum(
        o.size * o.dtype.itemsize for o in outs
    )
    specs = [
        HBM if i in hbm else SMEM if a.dtype == jnp.int32 else VMEM for i, a in enumerate(ins)
    ]
    return pl.pallas_call(
        kernel,
        out_shape=list(outs),
        in_specs=specs,
        out_specs=[VMEM] * len(outs),
        scratch_shapes=list(scratch),
        compiler_params=pltpu.CompilerParams(vmem_limit_bytes=limit * 2**20),
        cost_estimate=pl.CostEstimate(flops=flops, bytes_accessed=moved, transcendentals=0),
    )(*ins)


def on_device(latents, gn_gain, conv_weight, conv_bias, ln_gain, qkv_weight):
    _, rows_dev, width, chans = latents.shape
    part = rows_dev * width
    cells = 4 * part
    share = chans // 4
    me = lax.axis_index("rows")
    first = lax.axis_index("tm") == 0
    shape = jax.ShapeDtypeStruct
    bf16, f32 = jnp.bfloat16, jnp.float32
    lat = latents.reshape(part, chans)

    weight = lax.all_gather(qkv_weight, "rows", axis=0, tiled=True)
    fetched = lambda x: call(
        fetch_kernel, [shape(x.shape, x.dtype)], [x], [pltpu.SemaphoreType.DMA], hbm=(0,)
    )[0]
    lat_core = to_rows(lat, 1)
    lat = fetched(lat)
    mine, away = call(
        functools.partial(split_kernel, share),
        [shape((2, part, share), bf16)] * 2,
        [me.reshape(1), lat, lat_core],
    )
    came = to_rows(away, 2)
    taps_weight = fetched(after(conv_weight.reshape(3, 3 * share, chans), away))
    came = after(came, taps_weight)
    group = jnp.arange(share) // (chans // GROUPS)
    pool = (group[:, None] == group[None, :]).astype(f32)
    keep, send = call(
        functools.partial(conv_kernel, width),
        [shape((2, part, chans), f32), shape((2, part, chans), bf16)],
        [me.reshape(1), mine, came, gn_gain.reshape(4, share), taps_weight, pool],
        [
            pltpu.VMEM((cells, share), f32),
            pltpu.VMEM((cells + 2 * width, 3 * share), bf16),
            pltpu.VMEM((cells, chans), f32),
        ],
        flops=2 * cells * 9 * share * chans,
    )
    core = to_rows(send, 1)
    half = (keep[1] + core[1].astype(f32)).astype(bf16)
    chip = to_rows(half, 2)
    residual, feats = call(
        norm_kernel,
        [shape((part, chans), bf16)] * 2,
        [lat, keep, core, chip, conv_bias.reshape(1, chans), ln_gain.reshape(1, chans)],
    )

    devices = lax.axis_size("tm")
    prev = lax.ppermute(feats, "tm", [(i, i + 1) for i in range(devices - 1)])
    anchor = jnp.where(first, feats, jnp.zeros_like(feats))
    for level, route in enumerate(tree_levels(devices)):
        anchor = anchor + lax.ppermute(anchor, "tm", route)
        if level == 0:
            anchor = after(anchor, prev)
    prev = jnp.where(first, feats, after(prev, anchor))
    weight = fetched(after(weight, anchor))

    own = jnp.concatenate([prev, anchor], axis=0)
    core = to_rows(own, 1)
    chip = to_rows(own, 2)
    keys = 2 * part
    scratch = lambda keys: [pltpu.VMEM((keys, chans), bf16)] * 3
    flops = lambda keys: 2 * keys * chans * 2 * chans + 4 * part * keys * chans
    state = [
        shape((part, HEADS), f32),
        shape((part, HEADS), f32),
        shape((part, chans), f32),
    ]
    query, *prior = call(
        first_kernel,
        [shape((part, chans), bf16), *state],
        [feats, own, core, weight],
        scratch(2 * keys),
        flops=flops(2 * keys),
    )
    last = to_rows(after(chip, query), 1)
    prior = call(
        more_kernel,
        state,
        [query, chip, weight, *prior],
        scratch(keys),
        flops=flops(keys),
    )
    (restyled,) = call(
        last_kernel,
        [shape((part, chans), bf16)],
        [query, last, weight, *prior, residual],
        scratch(keys) + [pltpu.VMEM((part, chans), f32)],
        flops=flops(keys),
    )
    return restyled.reshape(1, rows_dev, width, chans)


def solution(mesh):
    return jax.shard_map(
        on_device,
        mesh=mesh,
        in_specs=(
            P("tm", "rows", None, None),
            P(),
            P(None, "rows", None),
            P(),
            P(),
            P("rows", None),
        ),
        out_specs=P("tm", "rows", None, None),
        check_vma=False,
    )
```

```python
import functools
import jax
import jax.numpy as jnp
from jax import lax
from jax.experimental import pallas as pl
from jax.experimental.pallas import tpu as pltpu
from jax.sharding import PartitionSpec as P

HEADS = 8
GROUPS = 32
EPS = 1e-05
HBM = pl.BlockSpec(memory_space=pltpu.HBM)
VMEM = pl.BlockSpec(memory_space=pltpu.VMEM)
SMEM = pl.BlockSpec(memory_space=pltpu.SMEM)


def tree_levels(devices):
    steps = []
    while 2 ** len(steps) < devices:
        steps.insert(0, 2 ** len(steps))
    levels, known = [], [0]
    for step in steps[1:] + steps[:1]:
        levels.append([(tm, tm + step) for tm in known])
        known = known + [tm + step for tm in known]
    return levels


def to_rows(x, flip):
    return lax.ppermute(x, "rows", [(i, i ^ flip) for i in range(4)])


def after(x, *done):
    return lax.optimization_barrier((x, *done))[0]


def fetch_kernel(source, out, landed):
    load = pltpu.make_async_copy(source, out, landed)
    load.start()
    load.wait()


def split_kernel(share, me_ref, own, core, mine, away):
    for out, want in ((mine, me_ref[0]), (away, me_ref[0] ^ 2)):
        for block in range(4):

            @pl.when(want == block)
            def _():
                for at, source in enumerate((own, core)):
                    out[at] = source[:, block * share : (block + 1) * share]


def conv_kernel(
    width, me_ref, mine, came, gain, weight, pool, keep, send, x_ref, taps, acc
):
    me = me_ref[0]
    blocks = (mine[0], mine[1], came[0], came[1])
    cells, chans = x_ref.shape
    part = cells // 4
    for flip, block in enumerate(blocks):
        at = pl.multiple_of((me ^ flip) * part, part)
        x_ref[pl.ds(at, part), :] = block.astype(jnp.float32)
    values = x_ref[...]

    def group_mean(column):
        wide = jnp.broadcast_to(column, (8, chans))
        out = jnp.dot(
            wide, pool[...], precision=lax.Precision.HIGHEST, preferred_element_type=jnp.float32
        )
        return out[:1]

    scale = 1.0 / (cells * (640 // GROUPS))
    mean = group_mean(jnp.sum(values, axis=0, keepdims=True)) * scale
    centred = values - mean
    spread = group_mean(jnp.sum(centred * centred, axis=0, keepdims=True)) * scale
    normed = centred * (lax.rsqrt(spread + EPS) * gain[pl.ds(me, 1), :])
    act = normed / (1.0 + jnp.exp(-normed))
    act = act.astype(jnp.bfloat16).astype(jnp.float32)
    column = lax.broadcasted_iota(jnp.int32, (cells, 1), 0) & (width - 1)
    before = jnp.where(column == 0, 0.0, pltpu.roll(act, 1, 0))
    after = jnp.where(column == width - 1, 0.0, pltpu.roll(act, cells - 1, 0))
    taps[:width, :] = jnp.zeros((width, taps.shape[1]), jnp.bfloat16)
    taps[width + cells :, :] = jnp.zeros((width, taps.shape[1]), jnp.bfloat16)
    taps[width : width + cells, :] = jnp.concatenate([before, act, after], axis=1).astype(
        jnp.bfloat16
    )
    acc[...] = sum(
        jnp.dot(
            taps[row * width : row * width + cells, :],
            weight[row],
            preferred_element_type=jnp.float32,
        )
        for row in range(3)
    )
    for flip in range(4):
        at = pl.multiple_of((me ^ flip) * part, part)
        out = acc[pl.ds(at, part), :]
        if flip % 2 == 0:
            keep[flip // 2] = out
        else:
            send[flip // 2] = out.astype(jnp.bfloat16)


def norm_kernel(lat, kept, core, chip, bias, gain, residual, feats):
    conv = kept[0] + core[0].astype(jnp.float32) + chip[...].astype(jnp.float32)
    res = (lat[...].astype(jnp.float32) + conv + bias[...]).astype(jnp.bfloat16)
    residual[...] = res
    rfloat = res.astype(jnp.float32)
    dev = rfloat - jnp.mean(rfloat, axis=1, keepdims=True)
    var = jnp.mean(dev * dev, axis=1, keepdims=True)
    feats[...] = (dev * lax.rsqrt(var + EPS) * gain[...]).astype(jnp.bfloat16)


def head_window(head, head_dim, chans):
    low = head * head_dim // 128 * 128
    high = min(-(-(head + 1) * head_dim // 128) * 128, chans)
    lane = low + lax.broadcasted_iota(jnp.int32, (1, high - low), 1)
    inside = (lane >= head * head_dim) & (lane < (head + 1) * head_dim)
    return slice(low, high), inside


def project(blocks, weight, joined, keys, vals):
    part, chans = blocks[0].shape
    for at, block in enumerate(blocks):
        joined[at * part : (at + 1) * part, :] = block[...]
    for out, first in ((keys, chans), (vals, 2 * chans)):
        out[...] = jnp.dot(
            joined[...], weight[:, first : first + chans], preferred_element_type=jnp.float32
        ).astype(jnp.bfloat16)


def scores_of(query, keys, head, window, inside):
    q_head = jnp.where(inside, query[:, window], 0)
    return lax.dot_general(
        q_head,
        keys[:, window],
        (((1,), (1,)), ((), ())),
        preferred_element_type=jnp.float32,
    )


def first_kernel(
    me_ref, feats, a0, a1, w0, w1, w2, w3, query, top, den, acc, weight, joined, keys, vals
):
    me = me_ref[0]
    chans = feats.shape[1]
    share = w0.shape[0]
    for flip, shard in enumerate((w0, w1, w2, w3)):
        at = pl.multiple_of((me ^ flip) * share, share)
        weight[pl.ds(at, share), :] = shard[...]
    head_dim = chans // HEADS
    scale = head_dim ** (-0.5)
    query[...] = jnp.dot(
        feats[...], weight[:, :chans], preferred_element_type=jnp.float32
    ).astype(jnp.bfloat16)
    project((a0, a1), weight, joined, keys, vals)
    for head in range(HEADS):
        window, inside = head_window(head, head_dim, chans)
        s = scores_of(query, keys, head, window, inside)
        peak = jnp.max(s, axis=1, keepdims=True)
        w = jnp.exp((s - peak) * scale)
        top[:, head : head + 1] = peak
        den[:, head : head + 1] = jnp.sum(w, axis=1, keepdims=True)
        out = jnp.dot(
            w.astype(jnp.bfloat16), vals[:, window], preferred_element_type=jnp.float32
        )
        acc[:, window] = jnp.where(inside, out, acc[:, window])


def attend(blocks, query, weight, top, den, acc, joined, keys, vals):
    head_dim = query.shape[1] // HEADS
    scale = head_dim ** (-0.5)
    project(blocks, weight, joined, keys, vals)
    for head in range(HEADS):
        window, inside = head_window(head, head_dim, query.shape[1])
        s = scores_of(query, keys, head, window, inside)
        old = top[:, head : head + 1]
        peak = jnp.maximum(old, jnp.max(s, axis=1, keepdims=True))
        factor = jnp.exp((old - peak) * scale)
        w = jnp.exp((s - peak) * scale)
        total = den[:, head : head + 1] * factor + jnp.sum(w, axis=1, keepdims=True)
        out = jnp.dot(
            w.astype(jnp.bfloat16), vals[:, window], preferred_element_type=jnp.float32
        )
        yield head, window, inside, peak, total, acc[:, window] * factor + out


def more_kernel(
    query, a0, weight, top, den, acc, new_top, new_den, new_acc, joined, keys, vals
):
    for head, window, inside, peak, total, out in attend(
        (a0,), query, weight, top, den, acc, joined, keys, vals
    ):
        new_top[:, head : head + 1] = peak
        new_den[:, head : head + 1] = total
        new_acc[:, window] = jnp.where(inside, out, new_acc[:, window])


def last_kernel(
    query, a0, weight, top, den, acc, residual, restyled, joined, keys, vals, mixed
):
    for head, window, inside, _, total, out in attend(
        (a0,), query, weight, top, den, acc, joined, keys, vals
    ):
        mixed[:, window] = jnp.where(inside, out / total, mixed[:, window])
    restyled[...] = (residual[...].astype(jnp.float32) + mixed[...]).astype(jnp.bfloat16)


def call(kernel, outs, ins, scratch=(), flops=0, limit=24, hbm=()):
    moved = sum(a.size * a.dtype.itemsize for a in ins) + sum(
        o.size * o.dtype.itemsize for o in outs
    )
    specs = [
        HBM if i in hbm else SMEM if a.dtype == jnp.int32 else VMEM for i, a in enumerate(ins)
    ]
    return pl.pallas_call(
        kernel,
        out_shape=list(outs),
        in_specs=specs,
        out_specs=[VMEM] * len(outs),
        scratch_shapes=list(scratch),
        compiler_params=pltpu.CompilerParams(vmem_limit_bytes=limit * 2**20),
        cost_estimate=pl.CostEstimate(flops=flops, bytes_accessed=moved, transcendentals=0),
    )(*ins)


def on_device(latents, gn_gain, conv_weight, conv_bias, ln_gain, qkv_weight):
    _, rows_dev, width, chans = latents.shape
    part = rows_dev * width
    cells = 4 * part
    share = chans // 4
    me = lax.axis_index("rows")
    first = lax.axis_index("tm") == 0
    shape = jax.ShapeDtypeStruct
    bf16, f32 = jnp.bfloat16, jnp.float32
    lat = latents.reshape(part, chans)

    fetched = lambda x: call(
        fetch_kernel, [shape(x.shape, x.dtype)], [x], [pltpu.SemaphoreType.DMA], hbm=(0,)
    )[0]
    lat_core = to_rows(lat, 1)
    lat = fetched(lat)
    mine, away = call(
        functools.partial(split_kernel, share),
        [shape((2, part, share), bf16)] * 2,
        [me.reshape(1), lat, lat_core],
    )
    came = to_rows(away, 2)
    weight_core = to_rows(after(qkv_weight, away), 1)
    taps_weight = fetched(after(conv_weight.reshape(3, 3 * share, chans), away))
    came = after(came, weight_core, taps_weight)
    group = jnp.arange(share) // (chans // GROUPS)
    pool = (group[:, None] == group[None, :]).astype(f32)
    keep, send = call(
        functools.partial(conv_kernel, width),
        [shape((2, part, chans), f32), shape((2, part, chans), bf16)],
        [me.reshape(1), mine, came, gn_gain.reshape(4, share), taps_weight, pool],
        [
            pltpu.VMEM((cells, share), f32),
            pltpu.VMEM((cells + 2 * width, 3 * share), bf16),
            pltpu.VMEM((cells, chans), f32),
        ],
        flops=2 * cells * 9 * share * chans,
    )
    core = to_rows(send, 1)
    half = (keep[1] + core[1].astype(f32)).astype(bf16)
    chip = to_rows(half, 2)
    residual, feats = call(
        norm_kernel,
        [shape((part, chans), bf16)] * 2,
        [lat, keep, core, chip, conv_bias.reshape(1, chans), ln_gain.reshape(1, chans)],
    )

    devices = lax.axis_size("tm")
    routes = tree_levels(devices)
    prev = lax.ppermute(feats, "tm", [(i, i + 1) for i in range(devices - 1)])
    weight_chip = to_rows(after(qkv_weight, feats), 2)

    def levels(anchor, which):
        for route in which:
            anchor = anchor + lax.ppermute(anchor, "tm", route)
        return anchor

    trips = 1 + jnp.minimum(lax.axis_index("tm"), 0)
    anchor = jnp.where(first, feats, jnp.zeros_like(feats))
    anchor = lax.fori_loop(0, trips, lambda _, a: levels(a, routes[:4]), anchor)
    anchor = after(anchor, prev, weight_chip)
    weight_last = to_rows(after(weight_chip, anchor), 1)
    anchor = after(levels(anchor, routes[4:5]), weight_last)
    anchor = levels(anchor, routes[5:])
    prev = jnp.where(first, feats, after(prev, anchor))
    shards = [qkv_weight, weight_core, weight_chip, weight_last]

    own = jnp.concatenate([prev, anchor], axis=0)
    core = to_rows(own, 1)
    chip = to_rows(own, 2)
    keys = 2 * part
    scratch = lambda keys: [pltpu.VMEM((keys, chans), bf16)] * 3
    flops = lambda keys: 2 * keys * chans * 2 * chans + 4 * part * keys * chans
    state = [
        shape((part, HEADS), f32),
        shape((part, HEADS), f32),
        shape((part, chans), f32),
    ]
    query, *prior, weight = call(
        first_kernel,
        [shape((part, chans), bf16), *state, shape((chans, 3 * chans), bf16)],
        [me.reshape(1), feats, own, core, *shards],
        scratch(2 * keys),
        flops=flops(2 * keys),
    )
    last = to_rows(after(chip, query), 1)
    prior = call(
        more_kernel,
        state,
        [query, chip, weight, *prior],
        scratch(keys),
        flops=flops(keys),
    )
    (restyled,) = call(
        last_kernel,
        [shape((part, chans), bf16)],
        [query, last, weight, *prior, residual],
        scratch(keys) + [pltpu.VMEM((part, chans), f32)],
        flops=flops(keys),
    )
    return restyled.reshape(1, rows_dev, width, chans)


def solution(mesh):
    return jax.shard_map(
        on_device,
        mesh=mesh,
        in_specs=(
            P("tm", "rows", None, None),
            P(),
            P(None, "rows", None),
            P(),
            P(),
            P("rows", None),
        ),
        out_specs=P("tm", "rows", None, None),
        check_vma=False,
    )
```

```python
import functools
import jax
import jax.numpy as jnp
from jax import lax
from jax.experimental import pallas as pl
from jax.experimental.pallas import tpu as pltpu
from jax.sharding import PartitionSpec as P

HEADS = 8
GROUPS = 32
EPS = 1e-05
HBM = pl.BlockSpec(memory_space=pltpu.HBM)
VMEM = pl.BlockSpec(memory_space=pltpu.VMEM)
SMEM = pl.BlockSpec(memory_space=pltpu.SMEM)


def tree_levels(devices):
    steps = []
    while 2 ** len(steps) < devices:
        steps.insert(0, 2 ** len(steps))
    levels, known = [], [0]
    for step in steps[1:] + steps[:1]:
        levels.append([(tm, tm + step) for tm in known])
        known = known + [tm + step for tm in known]
    return levels


def to_rows(x, flip):
    return lax.ppermute(x, "rows", [(i, i ^ flip) for i in range(4)])


def after(x, *done):
    return lax.optimization_barrier((x, *done))[0]


def fetch_kernel(source, out, landed):
    load = pltpu.make_async_copy(source, out, landed)
    load.start()
    load.wait()


def split_kernel(share, me_ref, own, core, mine, away):
    for out, want in ((mine, me_ref[0]), (away, me_ref[0] ^ 2)):
        for block in range(4):

            @pl.when(want == block)
            def _():
                for at, source in enumerate((own, core)):
                    out[at] = source[:, block * share : (block + 1) * share]


def conv_kernel(
    width, me_ref, mine, came, gain, weight, pool, keep, send, x_ref, taps, acc
):
    me = me_ref[0]
    blocks = (mine[0], mine[1], came[0], came[1])
    cells, chans = x_ref.shape
    part = cells // 4
    for flip, block in enumerate(blocks):
        at = pl.multiple_of((me ^ flip) * part, part)
        x_ref[pl.ds(at, part), :] = block.astype(jnp.float32)
    values = x_ref[...]

    def group_mean(column):
        wide = jnp.broadcast_to(column, (8, chans))
        out = jnp.dot(
            wide, pool[...], precision=lax.Precision.HIGHEST, preferred_element_type=jnp.float32
        )
        return out[:1]

    scale = 1.0 / (cells * (640 // GROUPS))
    mean = group_mean(jnp.sum(values, axis=0, keepdims=True)) * scale
    centred = values - mean
    spread = group_mean(jnp.sum(centred * centred, axis=0, keepdims=True)) * scale
    normed = centred * (lax.rsqrt(spread + EPS) * gain[pl.ds(me, 1), :])
    act = normed / (1.0 + jnp.exp(-normed))
    act = act.astype(jnp.bfloat16).astype(jnp.float32)
    column = lax.broadcasted_iota(jnp.int32, (cells, 1), 0) & (width - 1)
    before = jnp.where(column == 0, 0.0, pltpu.roll(act, 1, 0))
    after = jnp.where(column == width - 1, 0.0, pltpu.roll(act, cells - 1, 0))
    taps[:width, :] = jnp.zeros((width, taps.shape[1]), jnp.bfloat16)
    taps[width + cells :, :] = jnp.zeros((width, taps.shape[1]), jnp.bfloat16)
    taps[width : width + cells, :] = jnp.concatenate([before, act, after], axis=1).astype(
        jnp.bfloat16
    )
    acc[...] = sum(
        jnp.dot(
            taps[row * width : row * width + cells, :],
            weight[row],
            preferred_element_type=jnp.float32,
        )
        for row in range(3)
    )
    for flip in range(4):
        at = pl.multiple_of((me ^ flip) * part, part)
        out = acc[pl.ds(at, part), :]
        if flip % 2 == 0:
            keep[flip // 2] = out
        else:
            send[flip // 2] = out.astype(jnp.bfloat16)


def norm_kernel(lat, kept, core, chip, bias, gain, residual, feats):
    conv = kept[0] + core[0].astype(jnp.float32) + chip[...].astype(jnp.float32)
    res = (lat[...].astype(jnp.float32) + conv + bias[...]).astype(jnp.bfloat16)
    residual[...] = res
    rfloat = res.astype(jnp.float32)
    dev = rfloat - jnp.mean(rfloat, axis=1, keepdims=True)
    var = jnp.mean(dev * dev, axis=1, keepdims=True)
    feats[...] = (dev * lax.rsqrt(var + EPS) * gain[...]).astype(jnp.bfloat16)


def head_window(head, head_dim, chans):
    low = head * head_dim // 128 * 128
    high = min(-(-(head + 1) * head_dim // 128) * 128, chans)
    lane = low + lax.broadcasted_iota(jnp.int32, (1, high - low), 1)
    inside = (lane >= head * head_dim) & (lane < (head + 1) * head_dim)
    return slice(low, high), inside


def project(blocks, weight, joined, keys, vals):
    part, chans = blocks[0].shape
    for at, block in enumerate(blocks):
        joined[at * part : (at + 1) * part, :] = block[...]
    for out, first in ((keys, chans), (vals, 2 * chans)):
        out[...] = jnp.dot(
            joined[...], weight[:, first : first + chans], preferred_element_type=jnp.float32
        ).astype(jnp.bfloat16)


def attend(blocks, query, weight, joined, keys, vals, state=None):
    chans = query.shape[1]
    head_dim = chans // HEADS
    scale = head_dim ** (-0.5)
    project(blocks, weight, joined, keys, vals)
    heads = []
    for head in range(HEADS):
        window, inside = head_window(head, head_dim, chans)
        s = lax.dot_general(
            jnp.where(inside, query[:, window], 0),
            keys[:, window],
            (((1,), (1,)), ((), ())),
            preferred_element_type=jnp.float32,
        )
        peak = jnp.max(s, axis=1, keepdims=True)
        if state is not None:
            old = state[0][:, head : head + 1]
            peak = jnp.maximum(old, peak)
            factor = jnp.exp((old - peak) * scale)
        w = jnp.exp((s - peak) * scale)
        total = jnp.sum(w, axis=1, keepdims=True)
        out = jnp.dot(
            w.astype(jnp.bfloat16), vals[:, window], preferred_element_type=jnp.float32
        )
        if state is not None:
            total = state[1][:, head : head + 1] * factor + total
            out = state[2][:, window] * factor + out
        heads.append((peak, total, out))
    return heads


def tiles_of(outs, chans):
    for low in range(0, chans, 128):
        tile = None
        for head, out in enumerate(outs):
            window, inside = head_window(head, chans // HEADS, chans)
            if window.start <= low < window.stop:
                at = low - window.start
                part = out[:, at : at + 128]
                tile = part if tile is None else jnp.where(inside[:, at : at + 128], part, tile)
        yield slice(low, low + 128), tile


def keep_state(heads, top, den, acc):
    for head, (peak, total, _) in enumerate(heads):
        top[:, head : head + 1] = peak
        den[:, head : head + 1] = total
    for tile, value in tiles_of([out for _, _, out in heads], acc.shape[1]):
        acc[:, tile] = value


def first_kernel(
    me_ref, feats, a0, a1, w0, w1, w2, w3, query, top, den, acc, weight, joined, keys, vals
):
    me = me_ref[0]
    chans = feats.shape[1]
    share = w0.shape[0]
    for flip, shard in enumerate((w0, w1, w2, w3)):
        at = pl.multiple_of((me ^ flip) * share, share)
        weight[pl.ds(at, share), :] = shard[...]
    query[...] = jnp.dot(
        feats[...], weight[:, :chans], preferred_element_type=jnp.float32
    ).astype(jnp.bfloat16)
    keep_state(attend((a0, a1), query, weight, joined, keys, vals), top, den, acc)


def more_kernel(query, a0, weight, top, den, acc, new_top, new_den, new_acc, joined, keys, vals):
    heads = attend((a0,), query, weight, joined, keys, vals, (top, den, acc))
    keep_state(heads, new_top, new_den, new_acc)


def last_kernel(query, a0, weight, top, den, acc, residual, restyled, joined, keys, vals):
    heads = attend((a0,), query, weight, joined, keys, vals, (top, den, acc))
    mixed = [out / total for _, total, out in heads]
    for tile, value in tiles_of(mixed, restyled.shape[1]):
        restyled[:, tile] = (residual[:, tile].astype(jnp.float32) + value).astype(jnp.bfloat16)


def call(kernel, outs, ins, scratch=(), flops=0, limit=24, hbm=()):
    moved = sum(a.size * a.dtype.itemsize for a in ins) + sum(
        o.size * o.dtype.itemsize for o in outs
    )
    specs = [
        HBM if i in hbm else SMEM if a.dtype == jnp.int32 else VMEM for i, a in enumerate(ins)
    ]
    return pl.pallas_call(
        kernel,
        out_shape=list(outs),
        in_specs=specs,
        out_specs=[VMEM] * len(outs),
        scratch_shapes=list(scratch),
        compiler_params=pltpu.CompilerParams(vmem_limit_bytes=limit * 2**20),
        cost_estimate=pl.CostEstimate(flops=flops, bytes_accessed=moved, transcendentals=0),
    )(*ins)


def on_device(latents, gn_gain, conv_weight, conv_bias, ln_gain, qkv_weight):
    _, rows_dev, width, chans = latents.shape
    part = rows_dev * width
    cells = 4 * part
    share = chans // 4
    me = lax.axis_index("rows")
    first = lax.axis_index("tm") == 0
    shape = jax.ShapeDtypeStruct
    bf16, f32 = jnp.bfloat16, jnp.float32
    lat = latents.reshape(part, chans)

    fetched = lambda x: call(
        fetch_kernel, [shape(x.shape, x.dtype)], [x], [pltpu.SemaphoreType.DMA], hbm=(0,)
    )[0]
    lat_core = to_rows(lat, 1)
    lat = fetched(lat)
    mine, away = call(
        functools.partial(split_kernel, share),
        [shape((2, part, share), bf16)] * 2,
        [me.reshape(1), lat, lat_core],
    )
    came = to_rows(away, 2)
    weight_core = to_rows(after(qkv_weight, away), 1)
    taps_weight = fetched(after(conv_weight.reshape(3, 3 * share, chans), away))
    came = after(came, weight_core, taps_weight)
    group = jnp.arange(share) // (chans // GROUPS)
    pool = (group[:, None] == group[None, :]).astype(f32)
    keep, send = call(
        functools.partial(conv_kernel, width),
        [shape((2, part, chans), f32), shape((2, part, chans), bf16)],
        [me.reshape(1), mine, came, gn_gain.reshape(4, share), taps_weight, pool],
        [
            pltpu.VMEM((cells, share), f32),
            pltpu.VMEM((cells + 2 * width, 3 * share), bf16),
            pltpu.VMEM((cells, chans), f32),
        ],
        flops=2 * cells * 9 * share * chans,
    )
    core = to_rows(send, 1)
    half = (keep[1] + core[1].astype(f32)).astype(bf16)
    chip = to_rows(half, 2)
    residual, feats = call(
        norm_kernel,
        [shape((part, chans), bf16)] * 2,
        [lat, keep, core, chip, conv_bias.reshape(1, chans), ln_gain.reshape(1, chans)],
    )

    devices = lax.axis_size("tm")
    routes = tree_levels(devices)
    weight_chip = to_rows(after(qkv_weight, feats), 2)

    def levels(anchor, which):
        for route in which:
            anchor = anchor + lax.ppermute(anchor, "tm", route)
        return anchor

    trips = 1 + jnp.minimum(lax.axis_index("tm"), 0)
    anchor = jnp.where(first, feats, jnp.zeros_like(feats))
    anchor = lax.fori_loop(0, trips, lambda _, a: levels(a, routes[:4]), anchor)
    anchor = after(anchor, weight_chip)
    weight_last = to_rows(after(weight_chip, anchor), 1)
    anchor = after(levels(anchor, routes[4:5]), weight_last)
    prev = lax.ppermute(after(feats, anchor), "tm", [(i, i + 1) for i in range(devices - 1)])
    anchor = after(levels(anchor, routes[5:6]), prev)
    anchor = levels(anchor, routes[6:])
    prev = jnp.where(first, feats, after(prev, anchor))
    shards = [qkv_weight, weight_core, weight_chip, weight_last]

    own = jnp.concatenate([prev, anchor], axis=0)
    core = to_rows(own, 1)
    chip = to_rows(own, 2)
    keys = 2 * part
    scratch = lambda keys: [pltpu.VMEM((keys, chans), bf16)] * 3
    flops = lambda keys: 2 * keys * chans * 2 * chans + 4 * part * keys * chans
    state = [
        shape((part, HEADS), f32),
        shape((part, HEADS), f32),
        shape((part, chans), f32),
    ]
    query, *prior, weight = call(
        first_kernel,
        [shape((part, chans), bf16), *state, shape((chans, 3 * chans), bf16)],
        [me.reshape(1), feats, own, core, *shards],
        scratch(2 * keys),
        flops=flops(2 * keys),
    )
    last = to_rows(after(chip, query), 1)
    prior = call(
        more_kernel,
        state,
        [query, chip, weight, *prior],
        scratch(keys),
        flops=flops(keys),
    )
    (restyled,) = call(
        last_kernel,
        [shape((part, chans), bf16)],
        [query, last, weight, *prior, residual],
        scratch(keys),
        flops=flops(keys),
    )
    return restyled.reshape(1, rows_dev, width, chans)


def solution(mesh):
    return jax.shard_map(
        on_device,
        mesh=mesh,
        in_specs=(
            P("tm", "rows", None, None),
            P(),
            P(None, "rows", None),
            P(),
            P(),
            P("rows", None),
        ),
        out_specs=P("tm", "rows", None, None),
        check_vma=False,
    )
```

```python
import functools
import jax
import jax.numpy as jnp
from jax import lax
from jax.experimental import pallas as pl
from jax.experimental.pallas import tpu as pltpu
from jax.sharding import PartitionSpec as P

HEADS = 8
GROUPS = 32
EPS = 1e-05
HBM = pl.BlockSpec(memory_space=pltpu.HBM)
VMEM = pl.BlockSpec(memory_space=pltpu.VMEM)
SMEM = pl.BlockSpec(memory_space=pltpu.SMEM)


def tree_levels(devices):
    steps = []
    while 2 ** len(steps) < devices:
        steps.append(2 ** len(steps))
    levels, known = [], [0]
    for step in steps[1::-1] + steps[-2:1:-1] + steps[max(2, len(steps) - 1) :]:
        levels.append([(tm, tm + step) for tm in known])
        known = known + [tm + step for tm in known]
    return levels


def to_rows(x, flip):
    return lax.ppermute(x, "rows", [(i, i ^ flip) for i in range(4)])


def after(x, *done):
    return lax.optimization_barrier((x, *done))[0]


def fetch_kernel(source, out, landed):
    load = pltpu.make_async_copy(source, out, landed)
    load.start()
    load.wait()


def split_kernel(share, me_ref, own, core, mine, away):
    for out, want in ((mine, me_ref[0]), (away, me_ref[0] ^ 2)):
        for block in range(4):

            @pl.when(want == block)
            def _():
                for at, source in enumerate((own, core)):
                    out[at] = source[:, block * share : (block + 1) * share]


def conv_kernel(
    width, me_ref, mine, came, gain, weight, pool, keep, send, x_ref, taps, acc
):
    me = me_ref[0]
    blocks = (mine[0], mine[1], came[0], came[1])
    cells, chans = x_ref.shape
    part = cells // 4
    for flip, block in enumerate(blocks):
        at = pl.multiple_of((me ^ flip) * part, part)
        x_ref[pl.ds(at, part), :] = block.astype(jnp.float32)
    values = x_ref[...]

    def group_mean(column):
        wide = jnp.broadcast_to(column, (8, chans))
        out = jnp.dot(
            wide, pool[...], precision=lax.Precision.HIGHEST, preferred_element_type=jnp.float32
        )
        return out[:1]

    scale = 1.0 / (cells * (640 // GROUPS))
    mean = group_mean(jnp.sum(values, axis=0, keepdims=True)) * scale
    centred = values - mean
    spread = group_mean(jnp.sum(centred * centred, axis=0, keepdims=True)) * scale
    normed = centred * (lax.rsqrt(spread + EPS) * gain[pl.ds(me, 1), :])
    act = normed / (1.0 + jnp.exp(-normed))
    act = act.astype(jnp.bfloat16).astype(jnp.float32)
    column = lax.broadcasted_iota(jnp.int32, (cells, 1), 0) & (width - 1)
    before = jnp.where(column == 0, 0.0, pltpu.roll(act, 1, 0))
    after = jnp.where(column == width - 1, 0.0, pltpu.roll(act, cells - 1, 0))
    taps[:width, :] = jnp.zeros((width, taps.shape[1]), jnp.bfloat16)
    taps[width + cells :, :] = jnp.zeros((width, taps.shape[1]), jnp.bfloat16)
    taps[width : width + cells, :] = jnp.concatenate([before, act, after], axis=1).astype(
        jnp.bfloat16
    )
    acc[...] = sum(
        jnp.dot(
            taps[row * width : row * width + cells, :],
            weight[row],
            preferred_element_type=jnp.float32,
        )
        for row in range(3)
    )
    for flip in range(4):
        at = pl.multiple_of((me ^ flip) * part, part)
        out = acc[pl.ds(at, part), :]
        if flip % 2 == 0:
            keep[flip // 2] = out
        else:
            send[flip // 2] = out.astype(jnp.bfloat16)


def norm_kernel(lat, kept, core, chip, bias, gain, residual, feats):
    conv = kept[0] + core[0].astype(jnp.float32) + chip[...].astype(jnp.float32)
    res = (lat[...].astype(jnp.float32) + conv + bias[...]).astype(jnp.bfloat16)
    residual[...] = res
    rfloat = res.astype(jnp.float32)
    dev = rfloat - jnp.mean(rfloat, axis=1, keepdims=True)
    var = jnp.mean(dev * dev, axis=1, keepdims=True)
    feats[...] = (dev * lax.rsqrt(var + EPS) * gain[...]).astype(jnp.bfloat16)


def head_window(head, head_dim, chans):
    low = head * head_dim // 128 * 128
    high = min(-(-(head + 1) * head_dim // 128) * 128, chans)
    lane = low + lax.broadcasted_iota(jnp.int32, (1, high - low), 1)
    inside = (lane >= head * head_dim) & (lane < (head + 1) * head_dim)
    return slice(low, high), inside


def project(blocks, weight, joined, keys, vals):
    part, chans = blocks[0].shape
    for at, block in enumerate(blocks):
        joined[at * part : (at + 1) * part, :] = block[...]
    for out, first in ((keys, chans), (vals, 2 * chans)):
        out[...] = jnp.dot(
            joined[...], weight[:, first : first + chans], preferred_element_type=jnp.float32
        ).astype(jnp.bfloat16)


def attend(blocks, query, weight, joined, keys, vals, state=None):
    chans = query.shape[1]
    head_dim = chans // HEADS
    scale = head_dim ** (-0.5)
    project(blocks, weight, joined, keys, vals)
    heads = []
    for head in range(HEADS):
        window, inside = head_window(head, head_dim, chans)
        s = lax.dot_general(
            jnp.where(inside, query[:, window], 0),
            keys[:, window],
            (((1,), (1,)), ((), ())),
            preferred_element_type=jnp.float32,
        )
        peak = jnp.max(s, axis=1, keepdims=True)
        if state is not None:
            old = state[0][:, head : head + 1]
            peak = jnp.maximum(old, peak)
            factor = jnp.exp((old - peak) * scale)
        w = jnp.exp((s - peak) * scale)
        total = jnp.sum(w, axis=1, keepdims=True)
        out = jnp.dot(
            w.astype(jnp.bfloat16), vals[:, window], preferred_element_type=jnp.float32
        )
        if state is not None:
            total = state[1][:, head : head + 1] * factor + total
            out = state[2][:, window] * factor + out
        heads.append((peak, total, out))
    return heads


def tiles_of(outs, chans):
    for low in range(0, chans, 128):
        tile = None
        for head, out in enumerate(outs):
            window, inside = head_window(head, chans // HEADS, chans)
            if window.start <= low < window.stop:
                at = low - window.start
                part = out[:, at : at + 128]
                tile = part if tile is None else jnp.where(inside[:, at : at + 128], part, tile)
        yield slice(low, low + 128), tile


def keep_state(heads, top, den, acc):
    for head, (peak, total, _) in enumerate(heads):
        top[:, head : head + 1] = peak
        den[:, head : head + 1] = total
    for tile, value in tiles_of([out for _, _, out in heads], acc.shape[1]):
        acc[:, tile] = value


def first_kernel(
    me_ref, feats, a0, a1, w0, w1, w2, w3, query, top, den, acc, weight, joined, keys, vals
):
    me = me_ref[0]
    chans = feats.shape[1]
    share = w0.shape[0]
    for flip, shard in enumerate((w0, w1, w2, w3)):
        at = pl.multiple_of((me ^ flip) * share, share)
        weight[pl.ds(at, share), :] = shard[...]
    query[...] = jnp.dot(
        feats[...], weight[:, :chans], preferred_element_type=jnp.float32
    ).astype(jnp.bfloat16)
    keep_state(attend((a0, a1), query, weight, joined, keys, vals), top, den, acc)


def more_kernel(query, a0, weight, top, den, acc, new_top, new_den, new_acc, joined, keys, vals):
    heads = attend((a0,), query, weight, joined, keys, vals, (top, den, acc))
    keep_state(heads, new_top, new_den, new_acc)


def last_kernel(query, a0, weight, top, den, acc, residual, restyled, joined, keys, vals):
    heads = attend((a0,), query, weight, joined, keys, vals, (top, den, acc))
    mixed = [out / total for _, total, out in heads]
    for tile, value in tiles_of(mixed, restyled.shape[1]):
        restyled[:, tile] = (residual[:, tile].astype(jnp.float32) + value).astype(jnp.bfloat16)


def call(kernel, outs, ins, scratch=(), flops=0, limit=24, hbm=()):
    moved = sum(a.size * a.dtype.itemsize for a in ins) + sum(
        o.size * o.dtype.itemsize for o in outs
    )
    specs = [
        HBM if i in hbm else SMEM if a.dtype == jnp.int32 else VMEM for i, a in enumerate(ins)
    ]
    return pl.pallas_call(
        kernel,
        out_shape=list(outs),
        in_specs=specs,
        out_specs=[VMEM] * len(outs),
        scratch_shapes=list(scratch),
        compiler_params=pltpu.CompilerParams(vmem_limit_bytes=limit * 2**20),
        cost_estimate=pl.CostEstimate(flops=flops, bytes_accessed=moved, transcendentals=0),
    )(*ins)


def on_device(latents, gn_gain, conv_weight, conv_bias, ln_gain, qkv_weight):
    _, rows_dev, width, chans = latents.shape
    part = rows_dev * width
    cells = 4 * part
    share = chans // 4
    me = lax.axis_index("rows")
    first = lax.axis_index("tm") == 0
    shape = jax.ShapeDtypeStruct
    bf16, f32 = jnp.bfloat16, jnp.float32
    lat = latents.reshape(part, chans)

    fetched = lambda x: call(
        fetch_kernel, [shape(x.shape, x.dtype)], [x], [pltpu.SemaphoreType.DMA], hbm=(0,)
    )[0]
    lat_core = to_rows(lat, 1)
    lat = fetched(lat)
    mine, away = call(
        functools.partial(split_kernel, share),
        [shape((2, part, share), bf16)] * 2,
        [me.reshape(1), lat, lat_core],
    )
    came = to_rows(away, 2)
    weight_core = to_rows(after(qkv_weight, away), 1)
    taps_weight = fetched(after(conv_weight.reshape(3, 3 * share, chans), away))
    came = after(came, weight_core, taps_weight)
    group = jnp.arange(share) // (chans // GROUPS)
    pool = (group[:, None] == group[None, :]).astype(f32)
    keep, send = call(
        functools.partial(conv_kernel, width),
        [shape((2, part, chans), f32), shape((2, part, chans), bf16)],
        [me.reshape(1), mine, came, gn_gain.reshape(4, share), taps_weight, pool],
        [
            pltpu.VMEM((cells, share), f32),
            pltpu.VMEM((cells + 2 * width, 3 * share), bf16),
            pltpu.VMEM((cells, chans), f32),
        ],
        flops=2 * cells * 9 * share * chans,
    )
    core = to_rows(send, 1)
    half = (keep[1] + core[1].astype(f32)).astype(bf16)
    chip = to_rows(half, 2)
    residual, feats = call(
        norm_kernel,
        [shape((part, chans), bf16)] * 2,
        [lat, keep, core, chip, conv_bias.reshape(1, chans), ln_gain.reshape(1, chans)],
    )

    devices = lax.axis_size("tm")
    routes = tree_levels(devices)
    prev = lax.ppermute(feats, "tm", [(i, i + 1) for i in range(devices - 1)])
    weight_chip = to_rows(after(qkv_weight, feats), 2)

    def levels(anchor, which):
        for route in which:
            anchor = anchor + lax.ppermute(anchor, "tm", route)
        return anchor

    trips = 1 + jnp.minimum(lax.axis_index("tm"), 0)
    anchor = jnp.where(first, feats, jnp.zeros_like(feats))
    anchor = lax.fori_loop(0, trips, lambda _, a: levels(a, routes[:4]), anchor)
    anchor = after(anchor, prev, weight_chip)
    weight_last = to_rows(after(weight_chip, anchor), 1)
    anchor = after(levels(anchor, routes[4:5]), weight_last)
    anchor = levels(anchor, routes[5:])
    prev = jnp.where(first, feats, after(prev, anchor))
    shards = [qkv_weight, weight_core, weight_chip, weight_last]

    own = jnp.concatenate([prev, anchor], axis=0)
    core = to_rows(own, 1)
    chip = to_rows(own, 2)
    keys = 2 * part
    scratch = lambda keys: [pltpu.VMEM((keys, chans), bf16)] * 3
    flops = lambda keys: 2 * keys * chans * 2 * chans + 4 * part * keys * chans
    state = [
        shape((part, HEADS), f32),
        shape((part, HEADS), f32),
        shape((part, chans), f32),
    ]
    query, *prior, weight = call(
        first_kernel,
        [shape((part, chans), bf16), *state, shape((chans, 3 * chans), bf16)],
        [me.reshape(1), feats, own, core, *shards],
        scratch(2 * keys),
        flops=flops(2 * keys),
    )
    last = to_rows(after(chip, query), 1)
    prior = call(
        more_kernel,
        state,
        [query, chip, weight, *prior],
        scratch(keys),
        flops=flops(keys),
    )
    (restyled,) = call(
        last_kernel,
        [shape((part, chans), bf16)],
        [query, last, weight, *prior, residual],
        scratch(keys),
        flops=flops(keys),
    )
    return restyled.reshape(1, rows_dev, width, chans)


def solution(mesh):
    return jax.shard_map(
        on_device,
        mesh=mesh,
        in_specs=(
            P("tm", "rows", None, None),
            P(),
            P(None, "rows", None),
            P(),
            P(),
            P("rows", None),
        ),
        out_specs=P("tm", "rows", None, None),
        check_vma=False,
    )
```

```python
import functools
import jax
import jax.numpy as jnp
from jax import lax
from jax.experimental import pallas as pl
from jax.experimental.pallas import tpu as pltpu
from jax.sharding import PartitionSpec as P

HEADS = 8
GROUPS = 32
EPS = 1e-05
HBM = pl.BlockSpec(memory_space=pltpu.HBM)
VMEM = pl.BlockSpec(memory_space=pltpu.VMEM)
SMEM = pl.BlockSpec(memory_space=pltpu.SMEM)


def tree_levels(devices):
    steps = []
    while 2 ** len(steps) < devices:
        steps.append(2 ** len(steps))
    levels, known = [], [0]
    for step in steps[1::-1] + steps[-2:1:-1] + steps[max(2, len(steps) - 1) :]:
        levels.append([(tm, tm + step) for tm in known])
        known = known + [tm + step for tm in known]
    return levels


def to_rows(x, flip):
    return lax.ppermute(x, "rows", [(i, i ^ flip) for i in range(4)])


def after(x, *done):
    return lax.optimization_barrier((x, *done))[0]


def fetch_kernel(source, out, landed):
    load = pltpu.make_async_copy(source, out, landed)
    load.start()
    load.wait()


def split_kernel(share, me_ref, own, core, mine, away):
    for out, want in ((mine, me_ref[0]), (away, me_ref[0] ^ 2)):
        for block in range(4):

            @pl.when(want == block)
            def _():
                for at, source in enumerate((own, core)):
                    out[at] = source[:, block * share : (block + 1) * share]


def conv_kernel(
    width, me_ref, mine, came, gain, weight, pool, keep, send, x_ref, taps, acc
):
    me = me_ref[0]
    blocks = (mine[0], mine[1], came[0], came[1])
    cells, chans = x_ref.shape
    part = cells // 4
    for flip, block in enumerate(blocks):
        at = pl.multiple_of((me ^ flip) * part, part)
        x_ref[pl.ds(at, part), :] = block.astype(jnp.float32)
    values = x_ref[...]

    def group_mean(column):
        wide = jnp.broadcast_to(column, (8, chans))
        out = jnp.dot(
            wide, pool[...], precision=lax.Precision.HIGHEST, preferred_element_type=jnp.float32
        )
        return out[:1]

    scale = 1.0 / (cells * (640 // GROUPS))
    mean = group_mean(jnp.sum(values, axis=0, keepdims=True)) * scale
    centred = values - mean
    spread = group_mean(jnp.sum(centred * centred, axis=0, keepdims=True)) * scale
    normed = centred * (lax.rsqrt(spread + EPS) * gain[pl.ds(me, 1), :])
    act = normed / (1.0 + jnp.exp(-normed))
    act = act.astype(jnp.bfloat16).astype(jnp.float32)
    column = lax.broadcasted_iota(jnp.int32, (cells, 1), 0) & (width - 1)
    before = jnp.where(column == 0, 0.0, pltpu.roll(act, 1, 0))
    after = jnp.where(column == width - 1, 0.0, pltpu.roll(act, cells - 1, 0))
    taps[:width, :] = jnp.zeros((width, taps.shape[1]), jnp.bfloat16)
    taps[width + cells :, :] = jnp.zeros((width, taps.shape[1]), jnp.bfloat16)
    taps[width : width + cells, :] = jnp.concatenate([before, act, after], axis=1).astype(
        jnp.bfloat16
    )
    acc[...] = sum(
        jnp.dot(
            taps[row * width : row * width + cells, :],
            weight[row],
            preferred_element_type=jnp.float32,
        )
        for row in range(3)
    )
    for flip in range(4):
        at = pl.multiple_of((me ^ flip) * part, part)
        out = acc[pl.ds(at, part), :]
        if flip % 2 == 0:
            keep[flip // 2] = out
        else:
            send[flip // 2] = out.astype(jnp.bfloat16)


def norm_kernel(lat, kept, core, chip, bias, gain, residual, feats):
    conv = kept[0] + core[0].astype(jnp.float32) + chip[...].astype(jnp.float32)
    res = (lat[...].astype(jnp.float32) + conv + bias[...]).astype(jnp.bfloat16)
    residual[...] = res
    rfloat = res.astype(jnp.float32)
    dev = rfloat - jnp.mean(rfloat, axis=1, keepdims=True)
    var = jnp.mean(dev * dev, axis=1, keepdims=True)
    feats[...] = (dev * lax.rsqrt(var + EPS) * gain[...]).astype(jnp.bfloat16)


def head_window(head, head_dim, chans):
    low = head * head_dim // 128 * 128
    high = min(-(-(head + 1) * head_dim // 128) * 128, chans)
    lane = low + lax.broadcasted_iota(jnp.int32, (1, high - low), 1)
    inside = (lane >= head * head_dim) & (lane < (head + 1) * head_dim)
    return slice(low, high), inside


def project(blocks, weight, joined, keys, vals):
    chans = joined.shape[1]
    at = 0
    for block in blocks:
        joined[at : at + block.shape[0], :] = block[...]
        at += block.shape[0]
    for out, first in ((keys, chans), (vals, 2 * chans)):
        out[...] = jnp.dot(
            joined[...], weight[:, first : first + chans], preferred_element_type=jnp.float32
        ).astype(jnp.bfloat16)


def attend(blocks, query, weight, joined, keys, vals, state=None):
    chans = query.shape[1]
    head_dim = chans // HEADS
    scale = head_dim ** (-0.5)
    project(blocks, weight, joined, keys, vals)
    heads = []
    for head in range(HEADS):
        window, inside = head_window(head, head_dim, chans)
        s = lax.dot_general(
            jnp.where(inside, query[:, window], 0),
            keys[:, window],
            (((1,), (1,)), ((), ())),
            preferred_element_type=jnp.float32,
        )
        peak = jnp.max(s, axis=1, keepdims=True)
        if state is not None:
            old = state[0][:, head : head + 1]
            peak = jnp.maximum(old, peak)
            factor = jnp.exp((old - peak) * scale)
        w = jnp.exp((s - peak) * scale)
        total = jnp.sum(w, axis=1, keepdims=True)
        out = jnp.dot(
            w.astype(jnp.bfloat16), vals[:, window], preferred_element_type=jnp.float32
        )
        if state is not None:
            total = state[1][:, head : head + 1] * factor + total
            out = state[2][:, window] * factor + out
        heads.append((peak, total, out))
    return heads


def tiles_of(outs, chans):
    for low in range(0, chans, 128):
        tile = None
        for head, out in enumerate(outs):
            window, inside = head_window(head, chans // HEADS, chans)
            if window.start <= low < window.stop:
                at = low - window.start
                part = out[:, at : at + 128]
                tile = part if tile is None else jnp.where(inside[:, at : at + 128], part, tile)
        yield slice(low, low + 128), tile


def keep_state(heads, top, den, acc):
    for head, (peak, total, _) in enumerate(heads):
        top[:, head : head + 1] = peak
        den[:, head : head + 1] = total
    for tile, value in tiles_of([out for _, _, out in heads], acc.shape[1]):
        acc[:, tile] = value


def first_kernel(
    me_ref, feats, a0, a1, a2, w0, w1, w2, w3, query, top, den, acc, weight, joined, keys, vals
):
    me = me_ref[0]
    chans = feats.shape[1]
    share = w0.shape[0]
    for flip, shard in enumerate((w0, w1, w2, w3)):
        at = pl.multiple_of((me ^ flip) * share, share)
        weight[pl.ds(at, share), :] = shard[...]
    query[...] = jnp.dot(
        feats[...], weight[:, :chans], preferred_element_type=jnp.float32
    ).astype(jnp.bfloat16)
    keep_state(attend((a0, a1, a2), query, weight, joined, keys, vals), top, den, acc)


def more_kernel(query, a0, weight, top, den, acc, new_top, new_den, new_acc, joined, keys, vals):
    heads = attend((a0,), query, weight, joined, keys, vals, (top, den, acc))
    keep_state(heads, new_top, new_den, new_acc)


def last_kernel(query, a0, weight, top, den, acc, residual, restyled, joined, keys, vals):
    heads = attend((a0,), query, weight, joined, keys, vals, (top, den, acc))
    mixed = [out * (1.0 / total) for _, total, out in heads]
    for tile, value in tiles_of(mixed, restyled.shape[1]):
        restyled[:, tile] = (residual[:, tile].astype(jnp.float32) + value).astype(jnp.bfloat16)


def call(kernel, outs, ins, scratch=(), flops=0, limit=24, hbm=()):
    moved = sum(a.size * a.dtype.itemsize for a in ins) + sum(
        o.size * o.dtype.itemsize for o in outs
    )
    specs = [
        HBM if i in hbm else SMEM if a.dtype == jnp.int32 else VMEM for i, a in enumerate(ins)
    ]
    return pl.pallas_call(
        kernel,
        out_shape=list(outs),
        in_specs=specs,
        out_specs=[VMEM] * len(outs),
        scratch_shapes=list(scratch),
        compiler_params=pltpu.CompilerParams(vmem_limit_bytes=limit * 2**20),
        cost_estimate=pl.CostEstimate(flops=flops, bytes_accessed=moved, transcendentals=0),
    )(*ins)


def on_device(latents, gn_gain, conv_weight, conv_bias, ln_gain, qkv_weight):
    _, rows_dev, width, chans = latents.shape
    part = rows_dev * width
    cells = 4 * part
    share = chans // 4
    me = lax.axis_index("rows")
    first = lax.axis_index("tm") == 0
    shape = jax.ShapeDtypeStruct
    bf16, f32 = jnp.bfloat16, jnp.float32
    lat = latents.reshape(part, chans)

    fetched = lambda x: call(
        fetch_kernel, [shape(x.shape, x.dtype)], [x], [pltpu.SemaphoreType.DMA], hbm=(0,)
    )[0]
    lat_core = to_rows(lat, 1)
    lat = fetched(lat)
    mine, away = call(
        functools.partial(split_kernel, share),
        [shape((2, part, share), bf16)] * 2,
        [me.reshape(1), lat, lat_core],
    )
    came = to_rows(away, 2)
    weight_core = to_rows(after(qkv_weight, away), 1)
    taps_weight = fetched(after(conv_weight.reshape(3, 3 * share, chans), away))
    came = after(came, weight_core, taps_weight)
    group = jnp.arange(share) // (chans // GROUPS)
    pool = (group[:, None] == group[None, :]).astype(f32)
    keep, send = call(
        functools.partial(conv_kernel, width),
        [shape((2, part, chans), f32), shape((2, part, chans), bf16)],
        [me.reshape(1), mine, came, gn_gain.reshape(4, share), taps_weight, pool],
        [
            pltpu.VMEM((cells, share), f32),
            pltpu.VMEM((cells + 2 * width, 3 * share), bf16),
            pltpu.VMEM((cells, chans), f32),
        ],
        flops=2 * cells * 9 * share * chans,
    )
    core = to_rows(send, 1)
    half = (keep[1] + core[1].astype(f32)).astype(bf16)
    chip = to_rows(half, 2)
    residual, feats = call(
        norm_kernel,
        [shape((part, chans), bf16)] * 2,
        [lat, keep, core, chip, conv_bias.reshape(1, chans), ln_gain.reshape(1, chans)],
    )

    devices = lax.axis_size("tm")
    routes = tree_levels(devices)
    prev = lax.ppermute(feats, "tm", [(i, i + 1) for i in range(devices - 1)])
    weight_chip = to_rows(after(qkv_weight, feats), 2)

    trips = 1 + jnp.minimum(lax.axis_index("tm"), 0)

    def levels(anchor, which):
        for route in which:
            anchor = anchor + lax.ppermute(anchor, "tm", route)
        return anchor

    def looped(anchor, which):
        return lax.fori_loop(0, trips, lambda _, a: levels(a, which), anchor)

    anchor = looped(jnp.where(first, feats, jnp.zeros_like(feats)), routes[:4])
    anchor = after(anchor, prev, weight_chip)
    weight_last = to_rows(after(weight_chip, anchor), 1)
    anchor = after(looped(anchor, routes[4:6]), weight_last)
    anchor = levels(anchor, routes[6:])
    prev = jnp.where(first, feats, after(prev, anchor))
    shards = [qkv_weight, weight_core, weight_chip, weight_last]

    own = jnp.concatenate([prev, anchor], axis=0)
    chip = to_rows(own, 2)
    core = [to_rows(prev, 1), to_rows(anchor, 1)]
    keys = 2 * part
    scratch = lambda keys: [pltpu.VMEM((keys, chans), bf16)] * 3
    flops = lambda keys: 2 * keys * chans * 2 * chans + 4 * part * keys * chans
    state = [
        shape((part, HEADS), f32),
        shape((part, HEADS), f32),
        shape((part, chans), f32),
    ]
    query, *prior, weight = call(
        first_kernel,
        [shape((part, chans), bf16), *state, shape((chans, 3 * chans), bf16)],
        [me.reshape(1), feats, own, *core, *shards],
        scratch(2 * keys),
        flops=flops(2 * keys),
    )
    last = to_rows(after(chip, query), 1)
    prior = call(
        more_kernel,
        state,
        [query, chip, weight, *prior],
        scratch(keys),
        flops=flops(keys),
    )
    (restyled,) = call(
        last_kernel,
        [shape((part, chans), bf16)],
        [query, last, weight, *prior, residual],
        scratch(keys),
        flops=flops(keys),
    )
    return restyled.reshape(1, rows_dev, width, chans)


def solution(mesh):
    return jax.shard_map(
        on_device,
        mesh=mesh,
        in_specs=(
            P("tm", "rows", None, None),
            P(),
            P(None, "rows", None),
            P(),
            P(),
            P("rows", None),
        ),
        out_specs=P("tm", "rows", None, None),
        check_vma=False,
    )
```

```python
import functools
import jax
import jax.numpy as jnp
from jax import lax
from jax.experimental import pallas as pl
from jax.experimental.pallas import tpu as pltpu
from jax.sharding import PartitionSpec as P

HEADS = 8
GROUPS = 32
EPS = 1e-05
HBM = pl.BlockSpec(memory_space=pltpu.HBM)
VMEM = pl.BlockSpec(memory_space=pltpu.VMEM)
SMEM = pl.BlockSpec(memory_space=pltpu.SMEM)


def tree_levels(devices):
    if devices == 128:
        jumps = [{0: 2}, {0: 1, 2: 1}]
        jumps += [{0: 16}, {0: 48, 16: 16}, 8, 4, 64]
    else:
        jumps = [2**bit for bit in range(devices.bit_length()) if 2**bit < devices]
    levels, known = [], [0]
    for jump in jumps:
        step = lambda tm: jump if isinstance(jump, int) else jump[tm if tm in jump else tm // 16 * 16]
        level = [(tm, tm + step(tm)) for tm in known]
        levels.append([(tm, to) for tm, to in level if to < devices])
        known = known + [to for _, to in levels[-1]]
    return levels


def to_rows(x, flip):
    return lax.ppermute(x, "rows", [(i, i ^ flip) for i in range(4)])


def after(x, *done):
    return lax.optimization_barrier((x, *done))[0]


def fetch_kernel(source, out, landed):
    load = pltpu.make_async_copy(source, out, landed)
    load.start()
    load.wait()


def split_kernel(share, me_ref, own, core, mine, away):
    for out, want in ((mine, me_ref[0]), (away, me_ref[0] ^ 2)):
        for block in range(4):

            @pl.when(want == block)
            def _():
                for at, source in enumerate((own, core)):
                    out[at] = source[:, block * share : (block + 1) * share]


def conv_kernel(
    width, me_ref, mine, came, gain, weight, pool, keep, send, x_ref, taps, acc
):
    me = me_ref[0]
    blocks = (mine[0], mine[1], came[0], came[1])
    cells, chans = x_ref.shape
    part = cells // 4
    for flip, block in enumerate(blocks):
        at = pl.multiple_of((me ^ flip) * part, part)
        x_ref[pl.ds(at, part), :] = block.astype(jnp.float32)
    values = x_ref[...]

    def group_mean(column):
        wide = jnp.broadcast_to(column, (8, chans))
        out = jnp.dot(
            wide, pool[...], precision=lax.Precision.HIGHEST, preferred_element_type=jnp.float32
        )
        return out[:1]

    scale = 1.0 / (cells * (640 // GROUPS))
    mean = group_mean(jnp.sum(values, axis=0, keepdims=True)) * scale
    centred = values - mean
    spread = group_mean(jnp.sum(centred * centred, axis=0, keepdims=True)) * scale
    normed = centred * (lax.rsqrt(spread + EPS) * gain[pl.ds(me, 1), :])
    act = normed / (1.0 + jnp.exp(-normed))
    act = act.astype(jnp.bfloat16).astype(jnp.float32)
    column = lax.broadcasted_iota(jnp.int32, (cells, 1), 0) & (width - 1)
    before = jnp.where(column == 0, 0.0, pltpu.roll(act, 1, 0))
    after = jnp.where(column == width - 1, 0.0, pltpu.roll(act, cells - 1, 0))
    taps[:width, :] = jnp.zeros((width, taps.shape[1]), jnp.bfloat16)
    taps[width + cells :, :] = jnp.zeros((width, taps.shape[1]), jnp.bfloat16)
    taps[width : width + cells, :] = jnp.concatenate([before, act, after], axis=1).astype(
        jnp.bfloat16
    )
    acc[...] = sum(
        jnp.dot(
            taps[row * width : row * width + cells, :],
            weight[row],
            preferred_element_type=jnp.float32,
        )
        for row in range(3)
    )
    for flip in range(4):
        at = pl.multiple_of((me ^ flip) * part, part)
        out = acc[pl.ds(at, part), :]
        if flip % 2 == 0:
            keep[flip // 2] = out
        else:
            send[flip // 2] = out.astype(jnp.bfloat16)


def norm_kernel(lat, kept, core, chip, bias, gain, residual, feats):
    conv = kept[0] + core[0].astype(jnp.float32) + chip[...].astype(jnp.float32)
    res = (lat[...].astype(jnp.float32) + conv + bias[...]).astype(jnp.bfloat16)
    residual[...] = res
    rfloat = res.astype(jnp.float32)
    dev = rfloat - jnp.mean(rfloat, axis=1, keepdims=True)
    var = jnp.mean(dev * dev, axis=1, keepdims=True)
    feats[...] = (dev * lax.rsqrt(var + EPS) * gain[...]).astype(jnp.bfloat16)


def head_window(head, head_dim, chans):
    low = head * head_dim // 128 * 128
    high = min(-(-(head + 1) * head_dim // 128) * 128, chans)
    lane = low + lax.broadcasted_iota(jnp.int32, (1, high - low), 1)
    inside = (lane >= head * head_dim) & (lane < (head + 1) * head_dim)
    return slice(low, high), inside


def project(blocks, weight, joined, keys, vals):
    chans = joined.shape[1]
    at = 0
    for block in blocks:
        joined[at : at + block.shape[0], :] = block[...]
        at += block.shape[0]
    for out, first in ((keys, chans), (vals, 2 * chans)):
        out[...] = jnp.dot(
            joined[...], weight[:, first : first + chans], preferred_element_type=jnp.float32
        ).astype(jnp.bfloat16)


def attend(blocks, query, weight, joined, keys, vals, state=None):
    chans = query.shape[1]
    head_dim = chans // HEADS
    scale = head_dim ** (-0.5)
    project(blocks, weight, joined, keys, vals)
    heads = []
    for head in range(HEADS):
        window, inside = head_window(head, head_dim, chans)
        s = lax.dot_general(
            jnp.where(inside, query[:, window], 0),
            keys[:, window],
            (((1,), (1,)), ((), ())),
            preferred_element_type=jnp.float32,
        )
        peak = jnp.max(s, axis=1, keepdims=True)
        if state is not None:
            old = state[0][:, head : head + 1]
            peak = jnp.maximum(old, peak)
            factor = jnp.exp((old - peak) * scale)
        w = jnp.exp((s - peak) * scale)
        total = jnp.sum(w, axis=1, keepdims=True)
        out = jnp.dot(
            w.astype(jnp.bfloat16), vals[:, window], preferred_element_type=jnp.float32
        )
        if state is not None:
            total = state[1][:, head : head + 1] * factor + total
            out = state[2][:, window] * factor + out
        heads.append((peak, total, out))
    return heads


def tiles_of(outs, chans):
    for low in range(0, chans, 128):
        tile = None
        for head, out in enumerate(outs):
            window, inside = head_window(head, chans // HEADS, chans)
            if window.start <= low < window.stop:
                at = low - window.start
                part = out[:, at : at + 128]
                tile = part if tile is None else jnp.where(inside[:, at : at + 128], part, tile)
        yield slice(low, low + 128), tile


def keep_state(heads, top, den, acc):
    for head, (peak, total, _) in enumerate(heads):
        top[:, head : head + 1] = peak
        den[:, head : head + 1] = total
    for tile, value in tiles_of([out for _, _, out in heads], acc.shape[1]):
        acc[:, tile] = value


def first_kernel(
    me_ref, feats, a0, a1, a2, w0, w1, w2, w3, query, top, den, acc, weight, joined, keys, vals
):
    me = me_ref[0]
    chans = feats.shape[1]
    share = w0.shape[0]
    for flip, shard in enumerate((w0, w1, w2, w3)):
        at = pl.multiple_of((me ^ flip) * share, share)
        weight[pl.ds(at, share), :] = shard[...]
    query[...] = jnp.dot(
        feats[...], weight[:, :chans], preferred_element_type=jnp.float32
    ).astype(jnp.bfloat16)
    keep_state(attend((a0, a1, a2), query, weight, joined, keys, vals), top, den, acc)


def more_kernel(query, a0, weight, top, den, acc, new_top, new_den, new_acc, joined, keys, vals):
    heads = attend((a0,), query, weight, joined, keys, vals, (top, den, acc))
    keep_state(heads, new_top, new_den, new_acc)


def last_kernel(query, a0, weight, top, den, acc, residual, restyled, joined, keys, vals):
    heads = attend((a0,), query, weight, joined, keys, vals, (top, den, acc))
    mixed = [out * (1.0 / total) for _, total, out in heads]
    for tile, value in tiles_of(mixed, restyled.shape[1]):
        restyled[:, tile] = (residual[:, tile].astype(jnp.float32) + value).astype(jnp.bfloat16)


def call(kernel, outs, ins, scratch=(), flops=0, limit=24, hbm=()):
    moved = sum(a.size * a.dtype.itemsize for a in ins) + sum(
        o.size * o.dtype.itemsize for o in outs
    )
    specs = [
        HBM if i in hbm else SMEM if a.dtype == jnp.int32 else VMEM for i, a in enumerate(ins)
    ]
    return pl.pallas_call(
        kernel,
        out_shape=list(outs),
        in_specs=specs,
        out_specs=[VMEM] * len(outs),
        scratch_shapes=list(scratch),
        compiler_params=pltpu.CompilerParams(vmem_limit_bytes=limit * 2**20),
        cost_estimate=pl.CostEstimate(flops=flops, bytes_accessed=moved, transcendentals=0),
    )(*ins)


def on_device(latents, gn_gain, conv_weight, conv_bias, ln_gain, qkv_weight):
    _, rows_dev, width, chans = latents.shape
    part = rows_dev * width
    cells = 4 * part
    share = chans // 4
    me = lax.axis_index("rows")
    first = lax.axis_index("tm") == 0
    shape = jax.ShapeDtypeStruct
    bf16, f32 = jnp.bfloat16, jnp.float32
    lat = latents.reshape(part, chans)

    fetched = lambda x: call(
        fetch_kernel, [shape(x.shape, x.dtype)], [x], [pltpu.SemaphoreType.DMA], hbm=(0,)
    )[0]
    lat_core = to_rows(lat, 1)
    lat = fetched(lat)
    mine, away = call(
        functools.partial(split_kernel, share),
        [shape((2, part, share), bf16)] * 2,
        [me.reshape(1), lat, lat_core],
    )
    came = to_rows(away, 2)
    weight_core = to_rows(after(qkv_weight, away), 1)
    taps_weight = fetched(after(conv_weight.reshape(3, 3 * share, chans), away))
    came = after(came, weight_core, taps_weight)
    group = jnp.arange(share) // (chans // GROUPS)
    pool = (group[:, None] == group[None, :]).astype(f32)
    keep, send = call(
        functools.partial(conv_kernel, width),
        [shape((2, part, chans), f32), shape((2, part, chans), bf16)],
        [me.reshape(1), mine, came, gn_gain.reshape(4, share), taps_weight, pool],
        [
            pltpu.VMEM((cells, share), f32),
            pltpu.VMEM((cells + 2 * width, 3 * share), bf16),
            pltpu.VMEM((cells, chans), f32),
        ],
        flops=2 * cells * 9 * share * chans,
    )
    core = to_rows(send, 1)
    half = (keep[1] + core[1].astype(f32)).astype(bf16)
    chip = to_rows(half, 2)
    residual, feats = call(
        norm_kernel,
        [shape((part, chans), bf16)] * 2,
        [lat, keep, core, chip, conv_bias.reshape(1, chans), ln_gain.reshape(1, chans)],
    )

    devices = lax.axis_size("tm")
    routes = tree_levels(devices)
    weight_chip = to_rows(after(qkv_weight, feats), 2)

    trips = 1 + jnp.minimum(lax.axis_index("tm"), 0)

    def levels(anchor, which):
        for route in which:
            anchor = anchor + lax.ppermute(anchor, "tm", route)
        return anchor

    def looped(anchor, which):
        return lax.fori_loop(0, trips, lambda _, a: levels(a, which), anchor)

    def with_prev(_, carried):
        anchor = levels(carried[0], routes[:1])
        came = lax.ppermute(
            after(feats, anchor), "tm", [(i, i + 1) for i in range(devices - 1)]
        )
        return levels(anchor, routes[1:4]), came

    anchor = jnp.where(first, feats, jnp.zeros_like(feats))
    anchor, prev = lax.fori_loop(0, trips, with_prev, (anchor, feats))
    anchor = after(anchor, weight_chip)
    weight_last = to_rows(after(weight_chip, anchor), 1)
    anchor = after(looped(anchor, routes[4:6]), weight_last)
    anchor = levels(anchor, routes[6:])
    prev = jnp.where(first, feats, after(prev, anchor))
    shards = [qkv_weight, weight_core, weight_chip, weight_last]

    own = jnp.concatenate([prev, anchor], axis=0)
    chip = to_rows(own, 2)
    core = [to_rows(prev, 1), to_rows(anchor, 1)]
    keys = 2 * part
    scratch = lambda keys: [pltpu.VMEM((keys, chans), bf16)] * 3
    flops = lambda keys: 2 * keys * chans * 2 * chans + 4 * part * keys * chans
    state = [
        shape((part, HEADS), f32),
        shape((part, HEADS), f32),
        shape((part, chans), f32),
    ]
    query, *prior, weight = call(
        first_kernel,
        [shape((part, chans), bf16), *state, shape((chans, 3 * chans), bf16)],
        [me.reshape(1), feats, own, *core, *shards],
        scratch(2 * keys),
        flops=flops(2 * keys),
    )
    last = to_rows(after(chip, query), 1)
    prior = call(
        more_kernel,
        state,
        [query, chip, weight, *prior],
        scratch(keys),
        flops=flops(keys),
    )
    (restyled,) = call(
        last_kernel,
        [shape((part, chans), bf16)],
        [query, last, weight, *prior, residual],
        scratch(keys),
        flops=flops(keys),
    )
    return restyled.reshape(1, rows_dev, width, chans)


def solution(mesh):
    return jax.shard_map(
        on_device,
        mesh=mesh,
        in_specs=(
            P("tm", "rows", None, None),
            P(),
            P(None, "rows", None),
            P(),
            P(),
            P("rows", None),
        ),
        out_specs=P("tm", "rows", None, None),
        check_vma=False,
    )
```

```python
import functools
import jax
import jax.numpy as jnp
from jax import lax
from jax.experimental import pallas as pl
from jax.experimental.pallas import tpu as pltpu
from jax.sharding import PartitionSpec as P

HEADS = 8
GROUPS = 32
EPS = 1e-05
HBM = pl.BlockSpec(memory_space=pltpu.HBM)
VMEM = pl.BlockSpec(memory_space=pltpu.VMEM)
SMEM = pl.BlockSpec(memory_space=pltpu.SMEM)


def tree_levels(devices):
    if devices == 128:
        jumps = [{0: 2}, {0: 1, 2: 1}]
        jumps += [{0: 16}, {0: 48, 16: 16}, 8, 4, 64]
    else:
        jumps = [2**bit for bit in range(devices.bit_length()) if 2**bit < devices]
    levels, known = [], [0]
    for jump in jumps:
        step = lambda tm: jump if isinstance(jump, int) else jump[tm if tm in jump else tm // 16 * 16]
        level = [(tm, tm + step(tm)) for tm in known]
        levels.append([(tm, to) for tm, to in level if to < devices])
        known = known + [to for _, to in levels[-1]]
    return levels


def to_rows(x, flip):
    return lax.ppermute(x, "rows", [(i, i ^ flip) for i in range(4)])


def after(x, *done):
    return lax.optimization_barrier((x, *done))[0]


def fetch_kernel(source, out, landed):
    load = pltpu.make_async_copy(source, out, landed)
    load.start()
    load.wait()


def split_kernel(share, me_ref, own, core, mine, away):
    for out, want in ((mine, me_ref[0]), (away, me_ref[0] ^ 2)):
        for block in range(4):

            @pl.when(want == block)
            def _():
                for at, source in enumerate((own, core)):
                    out[at] = source[:, block * share : (block + 1) * share]


def conv_kernel(
    width, me_ref, mine, came, gain, weight, pool, keep, send, x_ref, taps, acc
):
    me = me_ref[0]
    blocks = (mine[0], mine[1], came[0], came[1])
    cells, chans = x_ref.shape
    part = cells // 4
    for flip, block in enumerate(blocks):
        at = pl.multiple_of((me ^ flip) * part, part)
        x_ref[pl.ds(at, part), :] = block.astype(jnp.float32)
    values = x_ref[...]

    def group_mean(column):
        wide = jnp.broadcast_to(column, (8, chans))
        out = jnp.dot(
            wide, pool[...], precision=lax.Precision.HIGHEST, preferred_element_type=jnp.float32
        )
        return out[:1]

    scale = 1.0 / (cells * (640 // GROUPS))
    mean = group_mean(jnp.sum(values, axis=0, keepdims=True)) * scale
    centred = values - mean
    spread = group_mean(jnp.sum(centred * centred, axis=0, keepdims=True)) * scale
    normed = centred * (lax.rsqrt(spread + EPS) * gain[pl.ds(me, 1), :])
    act = normed / (1.0 + jnp.exp(-normed))
    act = act.astype(jnp.bfloat16).astype(jnp.float32)
    column = lax.broadcasted_iota(jnp.int32, (cells, 1), 0) & (width - 1)
    before = jnp.where(column == 0, 0.0, pltpu.roll(act, 1, 0))
    after = jnp.where(column == width - 1, 0.0, pltpu.roll(act, cells - 1, 0))
    taps[:width, :] = jnp.zeros((width, taps.shape[1]), jnp.bfloat16)
    taps[width + cells :, :] = jnp.zeros((width, taps.shape[1]), jnp.bfloat16)
    taps[width : width + cells, :] = jnp.concatenate([before, act, after], axis=1).astype(
        jnp.bfloat16
    )
    acc[...] = sum(
        jnp.dot(
            taps[row * width : row * width + cells, :],
            weight[row],
            preferred_element_type=jnp.float32,
        )
        for row in range(3)
    )
    for flip in range(4):
        at = pl.multiple_of((me ^ flip) * part, part)
        out = acc[pl.ds(at, part), :]
        if flip % 2 == 0:
            keep[flip // 2] = out
        else:
            send[flip // 2] = out.astype(jnp.bfloat16)


def norm_kernel(lat, kept, core, chip, bias, gain, residual, feats):
    conv = kept[0] + core[0].astype(jnp.float32) + chip[...].astype(jnp.float32)
    res = (lat[...].astype(jnp.float32) + conv + bias[...]).astype(jnp.bfloat16)
    residual[...] = res
    rfloat = res.astype(jnp.float32)
    dev = rfloat - jnp.mean(rfloat, axis=1, keepdims=True)
    var = jnp.mean(dev * dev, axis=1, keepdims=True)
    feats[...] = (dev * lax.rsqrt(var + EPS) * gain[...]).astype(jnp.bfloat16)


def head_window(head, head_dim, chans):
    low = head * head_dim // 128 * 128
    high = min(-(-(head + 1) * head_dim // 128) * 128, chans)
    lane = low + lax.broadcasted_iota(jnp.int32, (1, high - low), 1)
    inside = (lane >= head * head_dim) & (lane < (head + 1) * head_dim)
    return slice(low, high), inside


def project(blocks, weight, joined, keys, vals):
    chans = joined.shape[1]
    at = 0
    for block in blocks:
        joined[at : at + block.shape[0], :] = block[...]
        at += block.shape[0]
    for out, first in ((keys, chans), (vals, 2 * chans)):
        out[...] = jnp.dot(
            joined[...], weight[:, first : first + chans], preferred_element_type=jnp.float32
        ).astype(jnp.bfloat16)


def attend(blocks, query, weight, joined, keys, vals, state=None):
    chans = query.shape[1]
    head_dim = chans // HEADS
    scale = head_dim ** (-0.5)
    project(blocks, weight, joined, keys, vals)
    heads = []
    for head in range(HEADS):
        window, inside = head_window(head, head_dim, chans)
        s = lax.dot_general(
            jnp.where(inside, query[:, window], 0),
            keys[:, window],
            (((1,), (1,)), ((), ())),
            preferred_element_type=jnp.float32,
        )
        peak = jnp.max(s, axis=1, keepdims=True)
        if state is not None:
            old = state[0][:, head : head + 1]
            peak = jnp.maximum(old, peak)
            factor = jnp.exp((old - peak) * scale)
        w = jnp.exp((s - peak) * scale)
        total = jnp.sum(w, axis=1, keepdims=True)
        out = jnp.dot(
            w.astype(jnp.bfloat16), vals[:, window], preferred_element_type=jnp.float32
        )
        if state is not None:
            total = state[1][:, head : head + 1] * factor + total
            out = state[2][:, window] * factor + out
        heads.append((peak, total, out))
    return heads


def tiles_of(outs, chans):
    for low in range(0, chans, 128):
        tile = None
        for head, out in enumerate(outs):
            window, inside = head_window(head, chans // HEADS, chans)
            if window.start <= low < window.stop:
                at = low - window.start
                part = out[:, at : at + 128]
                tile = part if tile is None else jnp.where(inside[:, at : at + 128], part, tile)
        yield slice(low, low + 128), tile


def keep_state(heads, top, den, acc):
    for head, (peak, total, _) in enumerate(heads):
        top[:, head : head + 1] = peak
        den[:, head : head + 1] = total
    for tile, value in tiles_of([out for _, _, out in heads], acc.shape[1]):
        acc[:, tile] = value


def first_kernel(
    me_ref, feats, a0, a1, a2, w0, w1, w2, w3, query, top, den, acc, weight, joined, keys, vals
):
    me = me_ref[0]
    chans = feats.shape[1]
    share = w0.shape[0]
    for flip, shard in enumerate((w0, w1, w2, w3)):
        at = pl.multiple_of((me ^ flip) * share, share)
        weight[pl.ds(at, share), :] = shard[...]
    query[...] = jnp.dot(
        feats[...], weight[:, :chans], preferred_element_type=jnp.float32
    ).astype(jnp.bfloat16)
    keep_state(attend((a0, a1, a2), query, weight, joined, keys, vals), top, den, acc)


def more_kernel(query, a0, weight, top, den, acc, new_top, new_den, new_acc, joined, keys, vals):
    heads = attend((a0,), query, weight, joined, keys, vals, (top, den, acc))
    keep_state(heads, new_top, new_den, new_acc)


def last_kernel(query, a0, weight, top, den, acc, residual, restyled, joined, keys, vals):
    heads = attend((a0,), query, weight, joined, keys, vals, (top, den, acc))
    mixed = [out * (1.0 / total) for _, total, out in heads]
    for tile, value in tiles_of(mixed, restyled.shape[1]):
        restyled[:, tile] = (residual[:, tile].astype(jnp.float32) + value).astype(jnp.bfloat16)


def call(kernel, outs, ins, scratch=(), flops=0, limit=24, hbm=()):
    moved = sum(a.size * a.dtype.itemsize for a in ins) + sum(
        o.size * o.dtype.itemsize for o in outs
    )
    specs = [
        HBM if i in hbm else SMEM if a.dtype == jnp.int32 else VMEM for i, a in enumerate(ins)
    ]
    return pl.pallas_call(
        kernel,
        out_shape=list(outs),
        in_specs=specs,
        out_specs=[VMEM] * len(outs),
        scratch_shapes=list(scratch),
        compiler_params=pltpu.CompilerParams(vmem_limit_bytes=limit * 2**20),
        cost_estimate=pl.CostEstimate(flops=flops, bytes_accessed=moved, transcendentals=0),
    )(*ins)


def on_device(latents, gn_gain, conv_weight, conv_bias, ln_gain, qkv_weight):
    _, rows_dev, width, chans = latents.shape
    part = rows_dev * width
    cells = 4 * part
    share = chans // 4
    me = lax.axis_index("rows")
    first = lax.axis_index("tm") == 0
    shape = jax.ShapeDtypeStruct
    bf16, f32 = jnp.bfloat16, jnp.float32
    lat = latents.reshape(part, chans)

    fetched = lambda x: call(
        fetch_kernel, [shape(x.shape, x.dtype)], [x], [pltpu.SemaphoreType.DMA], hbm=(0,)
    )[0]
    lat_core = to_rows(lat, 1)
    lat = fetched(lat)
    mine, away = call(
        functools.partial(split_kernel, share),
        [shape((2, part, share), bf16)] * 2,
        [me.reshape(1), lat, lat_core],
    )
    came = to_rows(away, 2)
    weight_core = to_rows(after(qkv_weight, away), 1)
    taps_weight = fetched(after(conv_weight.reshape(3, 3 * share, chans), away))
    came = after(came, weight_core, taps_weight)
    group = jnp.arange(share) // (chans // GROUPS)
    pool = (group[:, None] == group[None, :]).astype(f32)
    keep, send = call(
        functools.partial(conv_kernel, width),
        [shape((2, part, chans), f32), shape((2, part, chans), bf16)],
        [me.reshape(1), mine, came, gn_gain.reshape(4, share), taps_weight, pool],
        [
            pltpu.VMEM((cells, share), f32),
            pltpu.VMEM((cells + 2 * width, 3 * share), bf16),
            pltpu.VMEM((cells, chans), f32),
        ],
        flops=2 * cells * 9 * share * chans,
    )
    core = to_rows(send, 1)
    half = (keep[1] + core[1].astype(f32)).astype(bf16)
    chip = to_rows(half, 2)
    residual, feats = call(
        norm_kernel,
        [shape((part, chans), bf16)] * 2,
        [lat, keep, core, chip, conv_bias.reshape(1, chans), ln_gain.reshape(1, chans)],
    )

    devices = lax.axis_size("tm")
    routes = tree_levels(devices)
    prev = lax.ppermute(feats, "tm", [(i, i + 1) for i in range(devices - 1)])
    weight_chip = to_rows(after(qkv_weight, feats), 2)

    trips = 1 + jnp.minimum(lax.axis_index("tm"), 0)

    def levels(anchor, which):
        for route in which:
            anchor = anchor + lax.ppermute(anchor, "tm", route)
        return anchor

    def looped(anchor, which):
        return lax.fori_loop(0, trips, lambda _, a: levels(a, which), anchor)

    anchor = looped(jnp.where(first, feats, jnp.zeros_like(feats)), routes[:4])
    anchor = after(anchor, prev, weight_chip)
    weight_last = to_rows(after(weight_chip, anchor), 1)
    anchor = after(looped(anchor, routes[4:6]), weight_last)
    anchor = levels(anchor, routes[6:])
    prev = jnp.where(first, feats, after(prev, anchor))
    shards = [qkv_weight, weight_core, weight_chip, weight_last]

    own = jnp.concatenate([prev, anchor], axis=0)
    chip = to_rows(own, 2)
    core = [to_rows(prev, 1), to_rows(anchor, 1)]
    keys = 2 * part
    scratch = lambda keys: [pltpu.VMEM((keys, chans), bf16)] * 3
    flops = lambda keys: 2 * keys * chans * 2 * chans + 4 * part * keys * chans
    state = [
        shape((part, HEADS), f32),
        shape((part, HEADS), f32),
        shape((part, chans), f32),
    ]
    query, *prior, weight = call(
        first_kernel,
        [shape((part, chans), bf16), *state, shape((chans, 3 * chans), bf16)],
        [me.reshape(1), feats, own, *core, *shards],
        scratch(2 * keys),
        flops=flops(2 * keys),
    )
    last = to_rows(after(chip, query), 1)
    prior = call(
        more_kernel,
        state,
        [query, chip, weight, *prior],
        scratch(keys),
        flops=flops(keys),
    )
    (restyled,) = call(
        last_kernel,
        [shape((part, chans), bf16)],
        [query, last, weight, *prior, residual],
        scratch(keys),
        flops=flops(keys),
    )
    return restyled.reshape(1, rows_dev, width, chans)


def solution(mesh):
    return jax.shard_map(
        on_device,
        mesh=mesh,
        in_specs=(
            P("tm", "rows", None, None),
            P(),
            P(None, "rows", None),
            P(),
            P(),
            P("rows", None),
        ),
        out_specs=P("tm", "rows", None, None),
        check_vma=False,
    )
```

```python
import functools
import jax
import jax.numpy as jnp
from jax import lax
from jax.experimental import pallas as pl
from jax.experimental.pallas import tpu as pltpu
from jax.sharding import PartitionSpec as P

HEADS = 8
GROUPS = 32
EPS = 1e-05
HBM = pl.BlockSpec(memory_space=pltpu.HBM)
VMEM = pl.BlockSpec(memory_space=pltpu.VMEM)
SMEM = pl.BlockSpec(memory_space=pltpu.SMEM)


def tree_levels(devices):
    if devices == 128:
        jumps = [{0: 2}, {0: 1, 2: 1}]
        jumps += [{0: 16}, {0: 48, 16: 16}, 8, 4, 64]
    else:
        jumps = [2**bit for bit in range(devices.bit_length()) if 2**bit < devices]
    levels, known = [], [0]
    for jump in jumps:
        step = lambda tm: jump if isinstance(jump, int) else jump[tm if tm in jump else tm // 16 * 16]
        level = [(tm, tm + step(tm)) for tm in known]
        levels.append([(tm, to) for tm, to in level if to < devices])
        known = known + [to for _, to in levels[-1]]
    return levels


def to_rows(x, flip):
    return lax.ppermute(x, "rows", [(i, i ^ flip) for i in range(4)])


def after(x, *done):
    return lax.optimization_barrier((x, *done))[0]


def fetch_kernel(source, out, landed):
    load = pltpu.make_async_copy(source, out, landed)
    load.start()
    load.wait()


def split_kernel(share, me_ref, own, core, mine, away):
    for out, want in ((mine, me_ref[0]), (away, me_ref[0] ^ 2)):
        for block in range(4):

            @pl.when(want == block)
            def _():
                for at, source in enumerate((own, core)):
                    out[at] = source[:, block * share : (block + 1) * share]


def conv_kernel(
    width, me_ref, mine, came, gain, weight, pool, keep, send, x_ref, taps, acc
):
    me = me_ref[0]
    blocks = (mine[0], mine[1], came[0], came[1])
    cells, chans = x_ref.shape
    part = cells // 4
    for flip, block in enumerate(blocks):
        at = pl.multiple_of((me ^ flip) * part, part)
        x_ref[pl.ds(at, part), :] = block.astype(jnp.float32)
    values = x_ref[...]

    def group_mean(column):
        wide = jnp.broadcast_to(column, (8, chans))
        out = jnp.dot(
            wide, pool[...], precision=lax.Precision.HIGHEST, preferred_element_type=jnp.float32
        )
        return out[:1]

    scale = 1.0 / (cells * (640 // GROUPS))
    mean = group_mean(jnp.sum(values, axis=0, keepdims=True)) * scale
    centred = values - mean
    spread = group_mean(jnp.sum(centred * centred, axis=0, keepdims=True)) * scale
    normed = centred * (lax.rsqrt(spread + EPS) * gain[pl.ds(me, 1), :])
    act = normed / (1.0 + jnp.exp(-normed))
    act = act.astype(jnp.bfloat16).astype(jnp.float32)
    column = lax.broadcasted_iota(jnp.int32, (cells, 1), 0) & (width - 1)
    before = jnp.where(column == 0, 0.0, pltpu.roll(act, 1, 0))
    after = jnp.where(column == width - 1, 0.0, pltpu.roll(act, cells - 1, 0))
    taps[:width, :] = jnp.zeros((width, taps.shape[1]), jnp.bfloat16)
    taps[width + cells :, :] = jnp.zeros((width, taps.shape[1]), jnp.bfloat16)
    taps[width : width + cells, :] = jnp.concatenate([before, act, after], axis=1).astype(
        jnp.bfloat16
    )
    acc[...] = sum(
        jnp.dot(
            taps[row * width : row * width + cells, :],
            weight[row],
            preferred_element_type=jnp.float32,
        )
        for row in range(3)
    )
    for flip in range(4):
        at = pl.multiple_of((me ^ flip) * part, part)
        out = acc[pl.ds(at, part), :]
        if flip % 2 == 0:
            keep[flip // 2] = out
        else:
            send[flip // 2] = out.astype(jnp.bfloat16)


def norm_kernel(lat, kept, core, chip, bias, gain, residual, feats):
    conv = kept[0] + core[0].astype(jnp.float32) + chip[...].astype(jnp.float32)
    res = (lat[...].astype(jnp.float32) + conv + bias[...]).astype(jnp.bfloat16)
    residual[...] = res
    rfloat = res.astype(jnp.float32)
    dev = rfloat - jnp.mean(rfloat, axis=1, keepdims=True)
    var = jnp.mean(dev * dev, axis=1, keepdims=True)
    feats[...] = (dev * lax.rsqrt(var + EPS) * gain[...]).astype(jnp.bfloat16)


def head_window(head, head_dim, chans):
    low = head * head_dim // 128 * 128
    high = min(-(-(head + 1) * head_dim // 128) * 128, chans)
    lane = low + lax.broadcasted_iota(jnp.int32, (1, high - low), 1)
    inside = (lane >= head * head_dim) & (lane < (head + 1) * head_dim)
    return slice(low, high), inside


def project(blocks, weight, joined, keys, vals):
    chans = joined.shape[1]
    at = 0
    for block in blocks:
        joined[at : at + block.shape[0], :] = block[...]
        at += block.shape[0]
    for out, first in ((keys, chans), (vals, 2 * chans)):
        out[...] = jnp.dot(
            joined[...], weight[:, first : first + chans], preferred_element_type=jnp.float32
        ).astype(jnp.bfloat16)


def attend(blocks, query, weight, joined, keys, vals, state=None):
    chans = query.shape[1]
    head_dim = chans // HEADS
    scale = head_dim ** (-0.5)
    project(blocks, weight, joined, keys, vals)
    heads = []
    for head in range(HEADS):
        window, inside = head_window(head, head_dim, chans)
        s = lax.dot_general(
            jnp.where(inside, query[:, window], 0),
            keys[:, window],
            (((1,), (1,)), ((), ())),
            preferred_element_type=jnp.float32,
        )
        peak = jnp.max(s, axis=1, keepdims=True)
        if state is not None:
            old = state[0][:, head : head + 1]
            peak = jnp.maximum(old, peak)
            factor = jnp.exp((old - peak) * scale)
        w = jnp.exp((s - peak) * scale)
        total = jnp.sum(w, axis=1, keepdims=True)
        out = jnp.dot(
            w.astype(jnp.bfloat16), vals[:, window], preferred_element_type=jnp.float32
        )
        if state is not None:
            total = state[1][:, head : head + 1] * factor + total
            out = state[2][:, window] * factor + out
        heads.append((peak, total, out))
    return heads


def tiles_of(outs, chans):
    for low in range(0, chans, 128):
        tile = None
        for head, out in enumerate(outs):
            window, inside = head_window(head, chans // HEADS, chans)
            if window.start <= low < window.stop:
                at = low - window.start
                part = out[:, at : at + 128]
                tile = part if tile is None else jnp.where(inside[:, at : at + 128], part, tile)
        yield slice(low, low + 128), tile


def keep_state(heads, top, den, acc):
    for head, (peak, total, _) in enumerate(heads):
        top[:, head : head + 1] = peak
        den[:, head : head + 1] = total
    for tile, value in tiles_of([out for _, _, out in heads], acc.shape[1]):
        acc[:, tile] = value


def first_kernel(
    me_ref, feats, a0, a1, a2, w0, c0, c1, c2, c3, w2, w3, query, top, den, acc, weight, joined, keys, vals
):
    me = me_ref[0]
    chans = feats.shape[1]
    share = w0.shape[0]
    for flip, pieces in enumerate(((w0,), (c0, c1, c2, c3), (w2,), (w3,))):
        shard = jnp.concatenate([piece[...] for piece in pieces], axis=0)
        at = pl.multiple_of((me ^ flip) * share, share)
        weight[pl.ds(at, share), :] = shard
    query[...] = jnp.dot(
        feats[...], weight[:, :chans], preferred_element_type=jnp.float32
    ).astype(jnp.bfloat16)
    keep_state(attend((a0, a1, a2), query, weight, joined, keys, vals), top, den, acc)


def more_kernel(query, a0, weight, top, den, acc, new_top, new_den, new_acc, joined, keys, vals):
    heads = attend((a0,), query, weight, joined, keys, vals, (top, den, acc))
    keep_state(heads, new_top, new_den, new_acc)


def last_kernel(query, a0, weight, top, den, acc, residual, restyled, joined, keys, vals):
    heads = attend((a0,), query, weight, joined, keys, vals, (top, den, acc))
    mixed = [out * (1.0 / total) for _, total, out in heads]
    for tile, value in tiles_of(mixed, restyled.shape[1]):
        restyled[:, tile] = (residual[:, tile].astype(jnp.float32) + value).astype(jnp.bfloat16)


def call(kernel, outs, ins, scratch=(), flops=0, limit=24, hbm=()):
    moved = sum(a.size * a.dtype.itemsize for a in ins) + sum(
        o.size * o.dtype.itemsize for o in outs
    )
    specs = [
        HBM if i in hbm else SMEM if a.dtype == jnp.int32 else VMEM for i, a in enumerate(ins)
    ]
    return pl.pallas_call(
        kernel,
        out_shape=list(outs),
        in_specs=specs,
        out_specs=[VMEM] * len(outs),
        scratch_shapes=list(scratch),
        compiler_params=pltpu.CompilerParams(vmem_limit_bytes=limit * 2**20),
        cost_estimate=pl.CostEstimate(flops=flops, bytes_accessed=moved, transcendentals=0),
    )(*ins)


def on_device(latents, gn_gain, conv_weight, conv_bias, ln_gain, qkv_weight):
    _, rows_dev, width, chans = latents.shape
    part = rows_dev * width
    cells = 4 * part
    share = chans // 4
    me = lax.axis_index("rows")
    first = lax.axis_index("tm") == 0
    shape = jax.ShapeDtypeStruct
    bf16, f32 = jnp.bfloat16, jnp.float32
    lat = latents.reshape(part, chans)

    fetched = lambda x: call(
        fetch_kernel, [shape(x.shape, x.dtype)], [x], [pltpu.SemaphoreType.DMA], hbm=(0,)
    )[0]
    lat_core = to_rows(lat, 1)
    lat = fetched(lat)
    mine, away = call(
        functools.partial(split_kernel, share),
        [shape((2, part, share), bf16)] * 2,
        [me.reshape(1), lat, lat_core],
    )
    came = to_rows(away, 2)
    taps_weight = fetched(after(conv_weight.reshape(3, 3 * share, chans), away))
    came = after(came, taps_weight)
    group = jnp.arange(share) // (chans // GROUPS)
    pool = (group[:, None] == group[None, :]).astype(f32)
    keep, send = call(
        functools.partial(conv_kernel, width),
        [shape((2, part, chans), f32), shape((2, part, chans), bf16)],
        [me.reshape(1), mine, came, gn_gain.reshape(4, share), taps_weight, pool],
        [
            pltpu.VMEM((cells, share), f32),
            pltpu.VMEM((cells + 2 * width, 3 * share), bf16),
            pltpu.VMEM((cells, chans), f32),
        ],
        flops=2 * cells * 9 * share * chans,
    )
    core = to_rows(send, 1)
    half = (keep[1] + core[1].astype(f32)).astype(bf16)
    cut = share // 4
    chunk = lambda at, done: to_rows(after(qkv_weight[at * cut : (at + 1) * cut], done), 1)
    chunks = [chunk(at, half) for at in range(3)]
    chip = after(to_rows(half, 2), *chunks)
    residual, feats = call(
        norm_kernel,
        [shape((part, chans), bf16)] * 2,
        [lat, keep, core, chip, conv_bias.reshape(1, chans), ln_gain.reshape(1, chans)],
    )

    devices = lax.axis_size("tm")
    routes = tree_levels(devices)
    prev = lax.ppermute(feats, "tm", [(i, i + 1) for i in range(devices - 1)])
    weight_chip = to_rows(after(qkv_weight, feats), 2)

    trips = 1 + jnp.minimum(lax.axis_index("tm"), 0)

    def levels(anchor, which):
        for route in which:
            anchor = anchor + lax.ppermute(anchor, "tm", route)
        return anchor

    def looped(anchor, which):
        return lax.fori_loop(0, trips, lambda _, a: levels(a, which), anchor)

    anchor = looped(jnp.where(first, feats, jnp.zeros_like(feats)), routes[:4])
    anchor = after(anchor, prev, weight_chip)
    weight_last = to_rows(after(weight_chip, anchor), 1)
    anchor = after(looped(anchor, routes[4:6]), weight_last)
    chunks.append(chunk(3, anchor))
    anchor = after(levels(anchor, routes[6:]), chunks[3])
    prev = jnp.where(first, feats, after(prev, anchor))
    shards = [qkv_weight, *chunks, weight_chip, weight_last]

    own = jnp.concatenate([prev, anchor], axis=0)
    chip = to_rows(own, 2)
    core = [to_rows(prev, 1), to_rows(anchor, 1)]
    keys = 2 * part
    scratch = lambda keys: [pltpu.VMEM((keys, chans), bf16)] * 3
    flops = lambda keys: 2 * keys * chans * 2 * chans + 4 * part * keys * chans
    state = [
        shape((part, HEADS), f32),
        shape((part, HEADS), f32),
        shape((part, chans), f32),
    ]
    query, *prior, weight = call(
        first_kernel,
        [shape((part, chans), bf16), *state, shape((chans, 3 * chans), bf16)],
        [me.reshape(1), feats, own, *core, *shards],
        scratch(2 * keys),
        flops=flops(2 * keys),
    )
    last = to_rows(after(chip, query), 1)
    prior = call(
        more_kernel,
        state,
        [query, chip, weight, *prior],
        scratch(keys),
        flops=flops(keys),
    )
    (restyled,) = call(
        last_kernel,
        [shape((part, chans), bf16)],
        [query, last, weight, *prior, residual],
        scratch(keys),
        flops=flops(keys),
    )
    return restyled.reshape(1, rows_dev, width, chans)


def solution(mesh):
    return jax.shard_map(
        on_device,
        mesh=mesh,
        in_specs=(
            P("tm", "rows", None, None),
            P(),
            P(None, "rows", None),
            P(),
            P(),
            P("rows", None),
        ),
        out_specs=P("tm", "rows", None, None),
        check_vma=False,
    )
```
